256 devices in a mesh: leaf: 8 (over x, core), ctx: 8 (over z), head: 4 (over y).
Axes of the slice: x: 4, y: 4, z: 8, core: 2. Of those that a mesh axis runs over, the one named last changes fastest.
Arguments:
- queries: bfloat16 [16384, 8192], P(('leaf', 'ctx'), 'head')
- inputs: bfloat16 [16384, 5120], P(('leaf', 'ctx'), 'head'), may hold values from -6 to 6
- key_weight: bfloat16 [5120, 1024], P(None, 'head'), may hold values from -0.078125 to 0.078125
- value_weight: bfloat16 [5120, 1024], P(None, 'head'), may hold values from -0.078125 to 0.078125
- parents: int32 [128], replicated, may hold values from -1 to 126, as said below
- tile_dest: int32 [512], replicated, may hold values from 0 to 511, as said below
Outputs:
- placed: bfloat16 [16384, 8192], P(('leaf', 'ctx'), 'head')
The draws below stay inside these ranges and needn't reach their ends.
Inputs may be any that keep to these rules, and one draw needn't show every extreme that they name: parents[0] = -1, every later segment's parent is an earlier segment, and the last segment's parent is the segment just before it. `tile_dest`: a permutation; the tiles of block b (tiles b * 8 to b * 8 + 7) go to blocks of the same group of 8 consecutive blocks; from one block to one block go at most 2 tiles, and exactly 2 for some pairs in every group.
All inputs are finite; a program needn't handle non-finite values.
Results may differ from the reference program's by a relative error of at most 0.006.
The reference program's roundings to bfloat16 on the way (of `keys`, `values` and `weights`) count: a program that leaves them out, or rounds other values in their place, can miss the bound.
Values may be sent and summed in bfloat16 or wider, within the bound.
No kernel may reach another device: no remote copies, remote signals or barrier semaphores. Data moves between devices by JAX's collectives and lax.ppermute only.
A program may use at most 128 MiB of HBM per device.

```python
import jax
import jax.numpy as jnp
from jax import lax

MODEL_WIDTH = 5120
QUERY_HEADS = 64
KEY_VALUE_HEADS = 8
HEAD_SIZE = 128
SEGMENT_TOKENS = 128
TPD = 8
CAP = 2
TILE = 32
TOKENS = 16384
NSEG = 128
NTILE = 512
N_CTX = 8


def draw_queries(key, part):
    key = jax.random.fold_in(key, 11)
    values = jax.random.normal(key, (TOKENS, QUERY_HEADS * HEAD_SIZE), jnp.float32)
    return values.astype(jnp.bfloat16)


def draw_parents(key, part):
    key = jax.random.fold_in(key, 5)
    second, third = jax.random.split(key, 2)
    index = jnp.arange(NSEG, dtype=jnp.int32)
    span = NSEG // 2
    begin = jax.random.randint(third, (), 1, NSEG - span + 1)
    earlier = jax.random.randint(second, (NSEG,), 0, jnp.maximum(index, 1))
    inside = (index >= begin) & (index < begin + span)
    chained = inside | (index == NSEG - 1)
    linked = jnp.where(chained, index - 1, earlier)
    return jnp.where(index == 0, -1, linked).astype(jnp.int32)


def draw_tile_dest(key, part):
    key = jax.random.fold_in(key, 7)
    width = TPD * N_CTX
    groups = NTILE // width

    def one_group(group_key, group_index):
        first, second, third, fourth = jax.random.split(group_key, 4)
        residues = jax.random.permutation(first, N_CTX)[:TPD // CAP]
        order = jax.random.permutation(second, TPD)
        shifts = residues[order // CAP]
        tile_order = jax.vmap(lambda k: jax.random.permutation(k, TPD))(jax.random.split(third, N_CTX))
        slot_order = jax.vmap(lambda k: jax.random.permutation(k, TPD))(jax.random.split(fourth, N_CTX))
        source = jnp.arange(N_CTX, dtype=jnp.int32)[:, None]
        target = (source + shifts[None, :]) % N_CTX
        ranks = jnp.broadcast_to(jnp.arange(TPD, dtype=jnp.int32)[None, :], (N_CTX, TPD))
        value = group_index * width + target * TPD + slot_order[target, ranks]
        position = source * TPD + tile_order
        table = jnp.zeros((width,), jnp.int32)
        return table.at[position.reshape(-1)].set(value.reshape(-1).astype(jnp.int32))
    token_rows = jax.vmap(one_group)(jax.random.split(key, groups), jnp.arange(groups, dtype=jnp.int32))
    return token_rows.reshape(-1).astype(jnp.int32)


def levels(key, shape, shards, low, largest):
    def one(axis_at, parts):
        heights = jax.random.uniform(jax.random.fold_in(jax.random.fold_in(key, 6), axis_at), (parts,), jnp.float32, low / len(shards), largest / len(shards))
        return jnp.repeat(jnp.exp(heights), shape[axis_at] // parts).reshape((-1,) + (1,) * (len(shape) - axis_at - 1))

    level = one(*shards[0])
    for cut in shards[1:]:
        level = level * one(*cut)
    return level


def noise(own_key, dims, scale, most, pieces=(), kind=jnp.bfloat16):
    factor_of = levels(own_key, dims, pieces, -0.22, 0.18) if pieces else 1.0
    result = jax.random.normal(own_key, dims, jnp.float32) * scale * factor_of
    return jnp.minimum(jnp.maximum(result, -most), most).astype(kind)


def setup_inputs(seed: int = 0) -> dict:
    key_of = jax.random.split(jax.random.key(seed), 7)
    queries = draw_queries(jax.random.fold_in(key_of[6], 71), 0)
    inputs = noise(key_of[1], (TOKENS, MODEL_WIDTH), 1.0, 6.0, ((0, 64), (1, 4)))
    key_weight = noise(key_of[2], (MODEL_WIDTH, KEY_VALUE_HEADS * HEAD_SIZE), MODEL_WIDTH ** -0.5, 0.078125, ((1, 4),))
    value_weight = noise(key_of[3], (MODEL_WIDTH, KEY_VALUE_HEADS * HEAD_SIZE), MODEL_WIDTH ** -0.5, 0.078125, ((1, 4),))
    parents = draw_parents(jax.random.fold_in(key_of[6], 71), 0)
    tile_dest = draw_tile_dest(jax.random.fold_in(key_of[6], 71), 0)
    return {"queries": queries, "inputs": inputs, "key_weight": key_weight, "value_weight": value_weight, "parents": parents, "tile_dest": tile_dest}


large_negative_fill = -1.0e30


def closure(parents, count):
    reach = (parents[:, None] == jnp.arange(count, dtype=jnp.int32)[None, :]).astype(jnp.float32)
    for level in range(count.bit_length()):
        reach = jnp.minimum(reach + jnp.dot(reach, reach, precision=lax.Precision.HIGHEST), 1.0)
    return reach


def reference(queries, inputs, key_weight, value_weight, parents, tile_dest):
    keys = jnp.dot(inputs, key_weight, preferred_element_type=jnp.float32).astype(jnp.bfloat16)
    values = jnp.dot(inputs, value_weight, preferred_element_type=jnp.float32).astype(jnp.bfloat16)
    ancestry = closure(parents, NSEG)
    query_group = QUERY_HEADS // KEY_VALUE_HEADS
    scale = 1.0 / (HEAD_SIZE ** 0.5)

    def one_segment(index):
        token_rows = lax.dynamic_slice_in_dim(queries, index * SEGMENT_TOKENS, SEGMENT_TOKENS, 0).astype(jnp.float32)
        head_count = token_rows.reshape(SEGMENT_TOKENS, KEY_VALUE_HEADS, query_group, HEAD_SIZE).transpose(1, 0, 2, 3).reshape(KEY_VALUE_HEADS, SEGMENT_TOKENS * query_group, HEAD_SIZE)
        qpos = index * SEGMENT_TOKENS + jnp.arange(SEGMENT_TOKENS, dtype=jnp.int32)

        def block_scores(other):
            key_tile_block = lax.dynamic_slice_in_dim(keys, other * SEGMENT_TOKENS, SEGMENT_TOKENS, 0).astype(jnp.float32)
            key_tile_block = key_tile_block.reshape(SEGMENT_TOKENS, KEY_VALUE_HEADS, HEAD_SIZE).transpose(1, 0, 2)
            scores = jnp.einsum("hqd,hkd->hqk", head_count, key_tile_block) * scale
            kpos = other * SEGMENT_TOKENS + jnp.arange(SEGMENT_TOKENS, dtype=jnp.int32)
            allowed = (ancestry[index, other] > 0) | ((other == index) & (kpos[None, :] <= qpos[:, None]))
            mask = jnp.broadcast_to(allowed[:, None, :], (SEGMENT_TOKENS, query_group, SEGMENT_TOKENS)).reshape(SEGMENT_TOKENS * query_group, SEGMENT_TOKENS)
            return scores, mask[None]

        def needed(other):
            return (ancestry[index, other] > 0) | (other == index)

        def max_step(top, other):
            def grow(top_now):
                scores, mask = block_scores(other)
                return jnp.maximum(top_now, jnp.max(jnp.where(mask, scores, large_negative_fill), axis=-1))
            return lax.cond(needed(other), grow, lambda top_now: top_now, top), None

        top_start_offset = jnp.full((KEY_VALUE_HEADS, SEGMENT_TOKENS * query_group), large_negative_fill, jnp.float32)
        top, _ = lax.scan(max_step, top_start_offset, jnp.arange(NSEG, dtype=jnp.int32))

        def sum_step(state, other):
            def grow(state_now):
                total, accum = state_now
                scores, mask = block_scores(other)
                weights = jnp.where(mask, jnp.exp(scores - top[..., None]), 0.0)
                rounded = lax.optimization_barrier(weights.astype(jnp.bfloat16)).astype(jnp.float32)
                value_tile_block = lax.dynamic_slice_in_dim(values, other * SEGMENT_TOKENS, SEGMENT_TOKENS, 0).astype(jnp.float32)
                value_tile_block = value_tile_block.reshape(SEGMENT_TOKENS, KEY_VALUE_HEADS, HEAD_SIZE).transpose(1, 0, 2)
                return total + jnp.sum(weights, axis=-1), accum + jnp.einsum("hqk,hkd->hqd", rounded, value_tile_block)
            return lax.cond(needed(other), grow, lambda state_now: state_now, state), None

        start_offset = (jnp.zeros((KEY_VALUE_HEADS, SEGMENT_TOKENS * query_group), jnp.float32), jnp.zeros((KEY_VALUE_HEADS, SEGMENT_TOKENS * query_group, HEAD_SIZE), jnp.float32))
        (total, accum), _ = lax.scan(sum_step, start_offset, jnp.arange(NSEG, dtype=jnp.int32))
        attention_output = accum / total[..., None]
        return attention_output.reshape(KEY_VALUE_HEADS, SEGMENT_TOKENS, query_group, HEAD_SIZE).transpose(1, 0, 2, 3).reshape(SEGMENT_TOKENS, QUERY_HEADS * HEAD_SIZE).astype(jnp.bfloat16)

    attended = lax.map(one_segment, jnp.arange(NSEG, dtype=jnp.int32)).reshape(NTILE, TILE, QUERY_HEADS * HEAD_SIZE)
    placed = jnp.zeros((NTILE, TILE, QUERY_HEADS * HEAD_SIZE), jnp.bfloat16).at[tile_dest].set(attended)
    return placed.reshape(TOKENS, QUERY_HEADS * HEAD_SIZE)
```

```python
import functools
import math

import jax
import jax.numpy as jnp
from jax import lax
from jax.experimental import pallas as pl
from jax.experimental.pallas import tpu as pltpu
from jax.sharding import PartitionSpec as P

HEAD = 128
GROUP = 8
SEG = 128
TILE = 32
TPD = 8
CAP = 2
NX, NZ, NY = 4, 8, 4
ROWS = TILE * GROUP
SCALE = math.log2(math.e) / math.sqrt(HEAD)
FILL = -1.2e31
MIB = 1 << 20

XP = [(2 * x + c, 2 * ((x + 1) % NX) + c) for x in range(NX) for c in range(2)]
XM = [(2 * x + c, 2 * ((x - 1) % NX) + c) for x in range(NX) for c in range(2)]
CS = [(i, i ^ 1) for i in range(2 * NX)]


def turn(n, by):
    return [(i, (i + by) % n) for i in range(n)]


ZP, ZM = turn(NZ, 1), turn(NZ, -1)
YP, YM = turn(NY, 1), turn(NY, -1)

smem = functools.partial(pl.BlockSpec, memory_space=pltpu.SMEM)
vmem = functools.partial(pl.BlockSpec, memory_space=pltpu.VMEM)


def pack_kernel(where, dest, q, *outs):
    sends, table, info = outs[:NZ], outs[NZ], outs[NZ + 1]
    leaf, ctx = where[0], where[1]
    device = leaf * NZ + ctx
    shifts = [((dest[device * TPD + j] >> 3) - ctx) & (NZ - 1) for j in range(TPD)]
    ranks = []
    for j in range(TPD):
        rank = jnp.int32(0)
        for i in range(j):
            rank = rank + (shifts[i] == shifts[j]).astype(jnp.int32)
        ranks.append(rank)
    for s in range(NZ):
        for r in range(CAP):
            pick = jnp.int32(0)
            for j in range(TPD):
                pick = jnp.where((shifts[j] == s) & (ranks[j] == r), j, pick)
            sends[s][r] = q[pl.ds(pl.multiple_of(pick * TILE, TILE), TILE), :]
    for s in range(NZ):
        base = (leaf * NZ + ((ctx - s) & (NZ - 1))) * TPD
        table[s * CAP] = jnp.int32(-1)
        table[s * CAP + 1] = jnp.int32(-1)

        def one(j, rank, s=s, base=base):
            to = dest[base + j]
            mine = (to >> 3) == device

            @pl.when(mine)
            def _():
                table[s * CAP + rank] = to & (TPD - 1)
                info[to & (TPD - 1)] = base + j

            return rank + mine.astype(jnp.int32)

        lax.fori_loop(0, TPD, one, jnp.int32(0))


def pack(where, dest, q):
    width = q.shape[1]
    outs = pl.pallas_call(
        pack_kernel,
        in_specs=[smem(), smem(), vmem()],
        out_specs=[vmem()] * NZ + [smem(), smem()],
        out_shape=[jax.ShapeDtypeStruct((CAP, TILE, width), q.dtype)] * NZ
        + [jax.ShapeDtypeStruct((NZ * CAP,), jnp.int32), jax.ShapeDtypeStruct((TPD,), jnp.int32)],
        compiler_params=pltpu.CompilerParams(vmem_limit_bytes=32 * MIB),
        cost_estimate=pl.CostEstimate(flops=0, bytes_accessed=3 * MIB, transcendentals=0),
        name="pack",
    )(where, dest, q)
    return outs[:NZ], outs[NZ], outs[NZ + 1]


def walk_kernel(parents, info, which, place, lists, counts):
    def tile(d, carry):
        def body(state):
            at, found = state[0], state[1:]
            mine = which[at]
            used = jnp.int32(0)
            for n in range(4):
                used = jnp.where(mine == n, found[n], used)
            lists[(mine * TPD + d) * 64 + used] = place[at]
            return (parents[at],) + tuple(
                found[n] + (mine == n).astype(jnp.int32) for n in range(4)
            )

        lists[4 * TPD * 64 + d] = place[info[d] >> 2]
        start = (parents[info[d] >> 2],) + (jnp.int32(0),) * 4
        state = lax.while_loop(lambda now: now[0] >= 0, body, start)
        for n in range(4):
            counts[n * TPD + d] = state[1 + n]
        return carry

    lax.fori_loop(0, TPD, tile, 0)


def walk(parents, info, which, place):
    return pl.pallas_call(
        walk_kernel,
        in_specs=[smem()] * 4,
        out_specs=[smem()] * 2,
        out_shape=[
            jax.ShapeDtypeStruct((4 * TPD * 64 + TPD,), jnp.int32),
            jax.ShapeDtypeStruct((4 * TPD,), jnp.int32),
        ],
        cost_estimate=pl.CostEstimate(flops=0, bytes_accessed=20 * MIB, transcendentals=0),
        name="walk",
    )(parents, info, which, place)


def unpack_kernel(table, *refs):
    came, out = refs[:NZ], refs[NZ]
    for s in range(NZ):

        def one(r, carry, s=s):
            d = table[s * CAP + r]

            @pl.when(d >= 0)
            def _():
                for g in range(2):
                    heads = [
                        came[s][r, :, pl.ds((g * GROUP + h) * HEAD, HEAD)] for h in range(GROUP)
                    ]
                    out[d, g] = jnp.concatenate(heads, axis=0).T

            return carry

        lax.fori_loop(0, CAP, one, 0)


def unpack(table, came):
    return pl.pallas_call(
        unpack_kernel,
        in_specs=[smem()] + [vmem()] * NZ,
        out_specs=vmem(),
        out_shape=jax.ShapeDtypeStruct((TPD, 2, HEAD, ROWS), jnp.bfloat16),
        compiler_params=pltpu.CompilerParams(vmem_limit_bytes=32 * MIB),
        cost_estimate=pl.CostEstimate(flops=0, bytes_accessed=6 * MIB, transcendentals=0),
        name="unpack",
    )(table, *came)


def project_kernel(where, own, before, after, far0, far1, wk, wv, out):
    y = where[2]
    depth = own.shape[1]
    half = far0.shape[0]

    def rows(by):
        at = (y + by) & (NY - 1)
        return pl.ds(pl.multiple_of(at * depth, depth), depth)

    def times(w):
        total = jnp.dot(own[...], w[rows(0), :], preferred_element_type=jnp.float32)
        total += jnp.dot(before[...], w[rows(NY - 1), :], preferred_element_type=jnp.float32)
        total += jnp.dot(after[...], w[rows(1), :], preferred_element_type=jnp.float32)
        far = jnp.concatenate([far0[...], far1[...]], axis=0)
        return total + jnp.dot(far, w[rows(2), :], preferred_element_type=jnp.float32)

    k = times(wk)
    v = times(wv)
    for n in range(2):
        out[n, 0:SEG, :] = k[n * SEG : (n + 1) * SEG].astype(out.dtype)
        for g in range(2):
            part = v[n * SEG : (n + 1) * SEG, g * HEAD : (g + 1) * HEAD]
            out[n, SEG : 2 * SEG, g * HEAD : (g + 1) * HEAD] = part.T.astype(out.dtype)


def project(where, own, before, after, far0, far1, wk, wv):
    return pl.pallas_call(
        project_kernel,
        in_specs=[smem()] + [vmem()] * 7,
        out_specs=vmem(),
        out_shape=jax.ShapeDtypeStruct((2, 2 * SEG, 2 * HEAD), jnp.bfloat16),
        compiler_params=pltpu.CompilerParams(vmem_limit_bytes=40 * MIB),
        cost_estimate=pl.CostEstimate(flops=2 * 256 * 5120 * 512, bytes_accessed=8 * MIB, transcendentals=0),
        name="project",
    )(where, own, before, after, far0, far1, wk, wv)


def attend_kernel(which, finish, lists, counts, info, qt, same, other, *refs):
    if finish:
        old_top, old_total, old_sum, out, top, total, acc = refs
    else:
        top, total, acc = refs

    def steps(d, w, spots, mask):
        ids = [d * 2 + g for g in range(2)]
        scores, news, drops, weights = [], [], [], []
        for g in range(2):
            k = [w[at, 0:SEG, g * HEAD : (g + 1) * HEAD] for at in spots]
            k = k[0] if len(k) == 1 else jnp.concatenate(k, axis=0)
            s = jnp.dot(k, qt[d, g], preferred_element_type=jnp.float32)
            scores.append(s if mask is None else jnp.where(mask, s, FILL))
        tops = [top[i] for i in ids]
        totals = [total[i] for i in ids]
        sums = [acc[i] for i in ids]
        for g in range(2):
            new = jnp.maximum(tops[g], jnp.max(scores[g], axis=0, keepdims=True))
            news.append(new)
            drops.append(jnp.exp2((tops[g] - new) * SCALE))
            e = jnp.exp2((scores[g] - new) * SCALE)
            totals[g] = totals[g] * drops[g] + jnp.sum(e, axis=0, keepdims=True)
            weights.append(e.astype(jnp.bfloat16))
        for g in range(2):
            v = [w[at, SEG : 2 * SEG, g * HEAD : (g + 1) * HEAD] for at in spots]
            v = v[0] if len(v) == 1 else jnp.concatenate(v, axis=1)
            sums[g] = sums[g] * drops[g] + jnp.dot(
                v, weights[g], preferred_element_type=jnp.float32
            )
        for g in range(2):
            top[ids[g]] = news[g]
            total[ids[g]] = totals[g]
            acc[ids[g]] = sums[g]

    def tile(d, carry):
        for g in range(2):
            i = d * 2 + g
            if finish:
                top[i], total[i], acc[i] = old_top[i], old_total[i], old_sum[i]
            else:
                top[i] = jnp.full((1, ROWS), FILL, jnp.float32)
                total[i] = jnp.zeros((1, ROWS), jnp.float32)
                acc[i] = jnp.zeros((HEAD, ROWS), jnp.float32)
        seg, quarter = info[d] >> 2, info[d] & 3

        @pl.when((seg & 1) == which)
        def _():
            key = lax.broadcasted_iota(jnp.int32, (SEG, ROWS), 0)
            token = lax.broadcasted_iota(jnp.int32, (SEG, ROWS), 1) & (TILE - 1)
            ok = key <= token + quarter * TILE
            steps(d, same, [lists[4 * TPD * 64 + d]], ok)

        for n, w in ((2 * which, same), (2 * which + 1, other)):
            base = (n * TPD + d) * 64
            count = counts[n * TPD + d]

            def pair(i, c, base=base, w=w):
                steps(d, w, [lists[base + 2 * i], lists[base + 2 * i + 1]], None)
                return c

            lax.fori_loop(0, count >> 1, pair, 0)

            @pl.when((count & 1) == 1)
            def _(base=base, w=w, count=count):
                steps(d, w, [lists[base + count - 1]], None)

        if finish:
            for g in range(2):
                i = d * 2 + g
                o = (acc[i] / total[i]).T.astype(out.dtype)
                for h in range(GROUP):
                    out[
                        pl.ds(pl.multiple_of(d * TILE, TILE), TILE),
                        (g * GROUP + h) * HEAD : (g * GROUP + h + 1) * HEAD,
                    ] = o[h * TILE : (h + 1) * TILE]
        return carry

    lax.fori_loop(0, TPD, tile, 0)


def attend(which, lists, counts, info, qt, same, other, state):
    finish = state is not None
    shapes = [
        jax.ShapeDtypeStruct((2 * TPD, 1, ROWS), jnp.float32),
        jax.ShapeDtypeStruct((2 * TPD, 1, ROWS), jnp.float32),
        jax.ShapeDtypeStruct((2 * TPD, HEAD, ROWS), jnp.float32),
    ]
    result = jax.ShapeDtypeStruct((TPD * TILE, 2 * GROUP * HEAD), jnp.bfloat16)
    return pl.pallas_call(
        functools.partial(attend_kernel, which, finish),
        in_specs=[smem()] * 3 + [vmem()] * (6 if finish else 3),
        out_specs=vmem() if finish else [vmem()] * 3,
        out_shape=result if finish else shapes,
        scratch_shapes=[pltpu.VMEM(a.shape, a.dtype) for a in shapes] if finish else [],
        compiler_params=pltpu.CompilerParams(vmem_limit_bytes=48 * MIB),
        cost_estimate=pl.CostEstimate(
            flops=4 * 256 * 16 * 128 * 128 * 32, bytes_accessed=10 * MIB, transcendentals=0
        ),
        name="attend",
    )(lists, counts, info, qt, same, other, *(state or ()))


def cat(*parts):
    return jnp.concatenate(parts, axis=0)


def ring_z(block):
    half = block.shape[0] // 2
    parts = [block]
    low = high = block
    for _ in range(3):
        low = lax.ppermute(low, "ctx", ZP)
        high = lax.ppermute(high, "ctx", ZM)
        parts += [low, high]
    parts += [lax.ppermute(low[:half], "ctx", ZP), lax.ppermute(high[half:], "ctx", ZM)]
    return cat(*parts)


def ring_x(block):
    half = block.shape[0] // 2
    low = lax.ppermute(block, "leaf", XP)
    high = lax.ppermute(block, "leaf", XM)
    return cat(
        block,
        low,
        high,
        lax.ppermute(low[:half], "leaf", XP),
        lax.ppermute(high[half:], "leaf", XM),
    )


def on_device(queries, inputs, key_weight, value_weight, parents, tile_dest):
    leaf, ctx, y = lax.axis_index("leaf"), lax.axis_index("ctx"), lax.axis_index("head")
    where = jnp.stack([leaf, ctx, y]).astype(jnp.int32)
    sends, table, info = pack(where, tile_dest, queries)

    half = inputs.shape[0] // 2
    before = lax.ppermute(inputs, "head", YP)
    after = lax.ppermute(inputs, "head", YM)
    far0 = lax.ppermute(before[:half], "head", YP)
    far1 = lax.ppermute(after[half:], "head", YM)
    came = [sends[0]] + [lax.ppermute(sends[s], "ctx", turn(NZ, s)) for s in range(1, NZ)]

    seg = jnp.arange(parents.shape[0], dtype=jnp.int32)
    block = seg >> 1
    from_leaf, from_z = block >> 3, block & (NZ - 1)
    z = (from_z - ctx) & (NZ - 1)
    z = jnp.where(z == 0, 0, jnp.where(z < 4, 2 * z, jnp.where(z == 4, 7, 2 * (NZ - z) - 1)))
    x = ((from_leaf >> 1) - (leaf >> 1)) & (NX - 1)
    x = jnp.where(x == 0, 0, jnp.where(x == 1, 2, jnp.where(x == 2, 3, 1)))
    place = jnp.where((seg & 1) == 0, x * NZ + z, z * NX + x)
    which = 2 * (seg & 1) + ((from_leaf ^ leaf) & 1)
    lists, counts = walk(parents, info, which, place)
    qt = unpack(table, came)

    kv = project(where, inputs, before, after, far0, far1, key_weight, value_weight)
    even = ring_x(ring_z(kv[0]))
    odd = ring_z(ring_x(kv[1]))
    even2 = lax.ppermute(even, "leaf", CS)
    odd2 = lax.ppermute(odd, "leaf", CS)

    def blocks(a):
        return a.reshape(NX * NZ, 2 * SEG, 2 * HEAD)

    state = attend(0, lists, counts, info, qt, blocks(even), blocks(even2), None)
    return attend(1, lists, counts, info, qt, blocks(odd), blocks(odd2), state)


def solution(mesh):
    in_specs = (
        P(("leaf", "ctx"), "head"),
        P(("leaf", "ctx"), "head"),
        P(None, "head"),
        P(None, "head"),
        P(),
        P(),
    )
    out_specs = P(("leaf", "ctx"), "head")
    return jax.shard_map(
        on_device, mesh=mesh, in_specs=in_specs, out_specs=out_specs, check_vma=False
    )
```

```python
import functools
import math

import jax
import jax.numpy as jnp
from jax import lax
from jax.experimental import pallas as pl
from jax.experimental.pallas import tpu as pltpu
from jax.sharding import PartitionSpec as P

HEAD = 128
GROUP = 8
SEG = 128
TILE = 32
TPD = 8
CAP = 2
NX, NZ, NY = 4, 8, 4
ROWS = TILE * GROUP
SCALE = math.log2(math.e) / math.sqrt(HEAD)
FILL = -1.2e31
MIB = 1 << 20
UNIT = 4
LIST = 64 + 2 * 8 + 8
PIECES = 10

XP = [(2 * x + c, 2 * ((x + 1) % NX) + c) for x in range(NX) for c in range(2)]
XM = [(2 * x + c, 2 * ((x - 1) % NX) + c) for x in range(NX) for c in range(2)]
CS = [(i, i ^ 1) for i in range(2 * NX)]


def turn(n, by):
    return [(i, (i + by) % n) for i in range(n)]


ZP, ZM = turn(NZ, 1), turn(NZ, -1)
YP, YM = turn(NY, 1), turn(NY, -1)

smem = functools.partial(pl.BlockSpec, memory_space=pltpu.SMEM)
vmem = functools.partial(pl.BlockSpec, memory_space=pltpu.VMEM)


def pack_kernel(where, dest, q, *outs):
    sends, table, info = outs[:NZ], outs[NZ], outs[NZ + 1]
    leaf, ctx = where[0], where[1]
    device = leaf * NZ + ctx
    shifts = [((dest[device * TPD + j] >> 3) - ctx) & (NZ - 1) for j in range(TPD)]
    ranks = []
    for j in range(TPD):
        rank = jnp.int32(0)
        for i in range(j):
            rank = rank + (shifts[i] == shifts[j]).astype(jnp.int32)
        ranks.append(rank)
    for s in range(NZ):
        for r in range(CAP):
            pick = jnp.int32(0)
            for j in range(TPD):
                pick = jnp.where((shifts[j] == s) & (ranks[j] == r), j, pick)
            sends[s][r] = q[pl.ds(pl.multiple_of(pick * TILE, TILE), TILE), :]
    for s in range(NZ):
        base = (leaf * NZ + ((ctx - s) & (NZ - 1))) * TPD
        table[s * CAP] = jnp.int32(-1)
        table[s * CAP + 1] = jnp.int32(-1)

        def one(j, rank, s=s, base=base):
            to = dest[base + j]
            mine = (to >> 3) == device

            @pl.when(mine)
            def _():
                table[s * CAP + rank] = to & (TPD - 1)
                info[to & (TPD - 1)] = base + j

            return rank + mine.astype(jnp.int32)

        lax.fori_loop(0, TPD, one, jnp.int32(0))


def pack(where, dest, q):
    width = q.shape[1]
    outs = pl.pallas_call(
        pack_kernel,
        in_specs=[smem(), smem(), vmem()],
        out_specs=[vmem()] * NZ + [smem(), smem()],
        out_shape=[jax.ShapeDtypeStruct((CAP, TILE, width), q.dtype)] * NZ
        + [jax.ShapeDtypeStruct((NZ * CAP,), jnp.int32), jax.ShapeDtypeStruct((TPD,), jnp.int32)],
        compiler_params=pltpu.CompilerParams(vmem_limit_bytes=32 * MIB),
        cost_estimate=pl.CostEstimate(flops=0, bytes_accessed=3 * MIB, transcendentals=0),
        name="pack",
    )(where, dest, q)
    return outs[:NZ], outs[NZ], outs[NZ + 1]


def walk_kernel(parents, info, place, lists, counts):
    def tile(d, carry):
        evens, odds = d * LIST, (TPD + d) * LIST

        def body(state):
            at, even, odd = state
            is_odd = at & 1
            lists[jnp.where(is_odd == 1, odd, even)] = place[at]
            return parents[at], even + 1 - is_odd, odd + is_odd

        _, even, odd = lax.while_loop(
            lambda now: now[0] >= 0, body, (info[d] >> 2, jnp.int32(evens), jnp.int32(odds))
        )
        counts[d] = even - evens
        counts[TPD + d] = odd - odds
        for n in range(3 * UNIT):
            lists[even + n] = jnp.int32(0)
            lists[odd + n] = jnp.int32(0)
        return carry

    lax.fori_loop(0, TPD, tile, 0)


def walk(parents, info, place):
    return pl.pallas_call(
        walk_kernel,
        in_specs=[smem()] * 3,
        out_specs=[smem()] * 2,
        out_shape=[
            jax.ShapeDtypeStruct((2 * TPD * LIST,), jnp.int32),
            jax.ShapeDtypeStruct((2 * TPD,), jnp.int32),
        ],
        cost_estimate=pl.CostEstimate(flops=0, bytes_accessed=20 * MIB, transcendentals=0),
        name="walk",
    )(parents, info, place)


def unpack_kernel(table, *refs):
    came, out = refs[:NZ], refs[NZ]
    for s in range(NZ):

        def one(r, carry, s=s):
            d = table[s * CAP + r]

            @pl.when(d >= 0)
            def _():
                for g in range(2):
                    heads = [
                        came[s][r, :, pl.ds((g * GROUP + h) * HEAD, HEAD)] for h in range(GROUP)
                    ]
                    out[d, g] = jnp.concatenate(heads, axis=0).T

            return carry

        lax.fori_loop(0, CAP, one, 0)


def unpack(table, came):
    return pl.pallas_call(
        unpack_kernel,
        in_specs=[smem()] + [vmem()] * NZ,
        out_specs=vmem(),
        out_shape=jax.ShapeDtypeStruct((TPD, 2, HEAD, ROWS), jnp.bfloat16),
        compiler_params=pltpu.CompilerParams(vmem_limit_bytes=32 * MIB),
        cost_estimate=pl.CostEstimate(flops=0, bytes_accessed=6 * MIB, transcendentals=0),
        name="unpack",
    )(table, *came)


def project_kernel(where, own, before, after, far0, far1, wk, wv, out):
    y = where[2]
    depth = own.shape[1]
    half = far0.shape[0]

    def rows(by):
        at = (y + by) & (NY - 1)
        return pl.ds(pl.multiple_of(at * depth, depth), depth)

    def times(w):
        total = jnp.dot(own[...], w[rows(0), :], preferred_element_type=jnp.float32)
        total += jnp.dot(before[...], w[rows(NY - 1), :], preferred_element_type=jnp.float32)
        total += jnp.dot(after[...], w[rows(1), :], preferred_element_type=jnp.float32)
        far = jnp.concatenate([far0[...], far1[...]], axis=0)
        return total + jnp.dot(far, w[rows(2), :], preferred_element_type=jnp.float32)

    out[0:SEG, :] = times(wk).astype(out.dtype)
    v = times(wv)
    for g in range(2):
        part = v[:, g * HEAD : (g + 1) * HEAD]
        out[SEG : 2 * SEG, g * HEAD : (g + 1) * HEAD] = part.T.astype(out.dtype)


def project(where, own, before, after, far0, far1, wk, wv):
    return pl.pallas_call(
        project_kernel,
        in_specs=[smem()] + [vmem()] * 7,
        out_specs=vmem(),
        out_shape=jax.ShapeDtypeStruct((2 * SEG, 2 * HEAD), jnp.bfloat16),
        compiler_params=pltpu.CompilerParams(vmem_limit_bytes=40 * MIB),
        cost_estimate=pl.CostEstimate(flops=2 * 128 * 5120 * 512, bytes_accessed=8 * MIB, transcendentals=0),
        name="project",
    )(where, own, before, after, far0, far1, wk, wv)


def attend_kernel(which, finish, lists, counts, info, qt, *refs):
    pieces, refs = refs[:PIECES], refs[PIECES:]
    if finish:
        old_top, old_total, old_sum, out = refs[:4]
        kv, score, peak, weight, sems, top, total, acc = refs[4:]
    else:
        top, total, acc = refs[:3]
        kv, score, peak, weight, sems = refs[3:]
    copies, at = [], 0
    for n, piece in enumerate(pieces):
        size = piece.shape[0]
        copies.append(pltpu.make_async_copy(piece, kv.at[pl.ds(at, size)], sems.at[n]))
        at += size
    for copy in copies:
        copy.start()
    for copy in copies:
        copy.wait()

    def keys(w, g):
        return kv[w, 0:SEG, g * HEAD : (g + 1) * HEAD]

    def tile(d, carry):
        base = (which * TPD + d) * LIST
        count = counts[which * TPD + d]
        ids = [d * 2 + g for g in range(2)]

        def spots(i):
            return [lists[base + i * UNIT + u] for u in range(UNIT)]

        def scores(places, limit=None):
            for g in range(2):
                k = jnp.concatenate([keys(w, g) for w in places], axis=0)
                s = jnp.dot(k, qt[d, g], preferred_element_type=jnp.float32)
                if limit is not None:
                    key = lax.broadcasted_iota(jnp.int32, (UNIT * SEG, ROWS), 0)
                    s = jnp.where((key <= limit) | (key >= SEG), s, FILL)
                score[g] = s
                for u in range(UNIT):
                    part = s[u * SEG : (u + 1) * SEG].reshape(SEG // 8, 8, ROWS)
                    peak[g, u] = jnp.max(part, axis=0)

        for g in range(2):
            i = ids[g]
            if finish:
                top[i], total[i], acc[i] = old_top[i], old_total[i], old_sum[i]
            else:
                top[i] = jnp.full((1, ROWS), FILL, jnp.float32)
                total[i] = jnp.zeros((1, ROWS), jnp.float32)
                acc[i] = jnp.zeros((HEAD, ROWS), jnp.float32)
            weight[g] = jnp.zeros_like(weight[g])
        seg, quarter = info[d] >> 2, info[d] & 3
        token = lax.broadcasted_iota(jnp.int32, (UNIT * SEG, ROWS), 1) & (TILE - 1)
        scores(spots(0), token + jnp.where((seg & 1) == which, quarter * TILE, SEG))
        def add(places, drops):
            for g in range(2):
                v = jnp.concatenate(
                    [kv[w, SEG : 2 * SEG, g * HEAD : (g + 1) * HEAD] for w in places], axis=1
                )
                acc[ids[g]] = acc[ids[g]] * drops[g] + jnp.dot(
                    v, weight[g], preferred_element_type=jnp.float32
                )

        def body(i, drops):
            later = spots(i + 1)
            pens = [jnp.where(i * UNIT + u < count, 0.0, 3e31) for u in range(UNIT)]
            result = []
            add(spots(jnp.maximum(i - 1, 0)), drops)
            for g in range(2):
                old = top[ids[g]]
                peaks = [
                    peak[g, u] - pens[u] for u in range(UNIT)
                ]
                peaks = jnp.max(functools.reduce(jnp.maximum, peaks), axis=0, keepdims=True)
                new = jnp.maximum(old, peaks)
                drop = jnp.exp2((old - new) * SCALE)
                part = jnp.zeros((8, ROWS), jnp.float32)
                for u in range(UNIT):
                    e = jnp.exp2((score[g, u * SEG : (u + 1) * SEG] - (new + pens[u])) * SCALE)
                    part += jnp.sum(e.reshape(SEG // 8, 8, ROWS), axis=0)
                    weight[g, u * SEG : (u + 1) * SEG] = e.astype(jnp.bfloat16)
                total[ids[g]] = total[ids[g]] * drop + jnp.sum(part, axis=0, keepdims=True)
                top[ids[g]] = new
                result.append(drop)
            scores(later)
            return tuple(result)

        rounds = (count + UNIT - 1) // UNIT
        ones = jnp.ones((1, ROWS), jnp.float32)
        drops = lax.fori_loop(0, rounds, body, (ones, ones))
        add(spots(jnp.maximum(rounds - 1, 0)), drops)

        if finish:
            for g in range(2):
                i = ids[g]
                o = (acc[i] / total[i]).T.astype(out.dtype)
                for h in range(GROUP):
                    out[
                        pl.ds(pl.multiple_of(d * TILE, TILE), TILE),
                        (g * GROUP + h) * HEAD : (g * GROUP + h + 1) * HEAD,
                    ] = o[h * TILE : (h + 1) * TILE]
        return carry

    lax.fori_loop(0, TPD, tile, 0)


def attend(which, lists, counts, info, qt, pieces, state):
    finish = state is not None
    shapes = [
        jax.ShapeDtypeStruct((2 * TPD, 1, ROWS), jnp.float32),
        jax.ShapeDtypeStruct((2 * TPD, 1, ROWS), jnp.float32),
        jax.ShapeDtypeStruct((2 * TPD, HEAD, ROWS), jnp.float32),
    ]
    result = jax.ShapeDtypeStruct((TPD * TILE, 2 * GROUP * HEAD), jnp.bfloat16)
    scratch = [
        pltpu.VMEM((2 * NX * NZ, 2 * SEG, 2 * HEAD), jnp.bfloat16),
        pltpu.VMEM((2, UNIT * SEG, ROWS), jnp.float32),
        pltpu.VMEM((2, UNIT, 8, ROWS), jnp.float32),
        pltpu.VMEM((2, UNIT * SEG, ROWS), jnp.bfloat16),
        pltpu.SemaphoreType.DMA((PIECES,)),
    ]
    if finish:
        scratch += [pltpu.VMEM(a.shape, a.dtype) for a in shapes]
    return pl.pallas_call(
        functools.partial(attend_kernel, which, finish),
        in_specs=[smem()] * 3
        + [vmem()]
        + [pl.BlockSpec(memory_space=pl.ANY)] * PIECES
        + [vmem()] * (3 if finish else 0),
        out_specs=vmem() if finish else [vmem()] * 3,
        out_shape=result if finish else shapes,
        scratch_shapes=scratch,
        compiler_params=pltpu.CompilerParams(vmem_limit_bytes=36 * MIB),
        cost_estimate=pl.CostEstimate(
            flops=4 * 256 * 16 * 128 * 128 * 32, bytes_accessed=10 * MIB, transcendentals=0
        ),
        name="attend",
    )(lists, counts, info, qt, *pieces, *(state or ()))


def cat(*parts):
    return jnp.concatenate(parts, axis=0)


def ring_z(block):
    half = block.shape[0] // 2
    parts = [block]
    low = high = block
    for _ in range(3):
        low = lax.ppermute(low, "ctx", ZP)
        high = lax.ppermute(high, "ctx", ZM)
        parts += [low, high]
    return parts + [lax.ppermute(low[:half], "ctx", ZP), lax.ppermute(high[half:], "ctx", ZM)]


def ring_x(block):
    half = block.shape[0] // 2
    low = lax.ppermute(block, "leaf", XP)
    high = lax.ppermute(block, "leaf", XM)
    far0 = lax.ppermute(low[:half], "leaf", XP)
    far1 = lax.ppermute(high[half:], "leaf", XM)
    return [block, low, high, far0, far1]


def gather_y(block):
    half = block.shape[0] // 2
    low = lax.ppermute(block, "head", YP)
    high = lax.ppermute(block, "head", YM)
    far0 = lax.ppermute(low[:half], "head", YP)
    far1 = lax.ppermute(high[half:], "head", YM)
    return [block, low, high, far0, far1]


def on_device(queries, inputs, key_weight, value_weight, parents, tile_dest):
    leaf, ctx, y = lax.axis_index("leaf"), lax.axis_index("ctx"), lax.axis_index("head")
    where = jnp.stack([leaf, ctx, y]).astype(jnp.int32)
    sends, table, info = pack(where, tile_dest, queries)
    came = [sends[0]] + [lax.ppermute(sends[s], "ctx", turn(NZ, s)) for s in range(1, NZ)]
    tokens = inputs.shape[0] // 2
    rows0 = gather_y(inputs[:tokens])
    rows1 = gather_y(inputs[tokens:])
    rows0, came[1], came[7] = lax.optimization_barrier((rows0, came[1], came[7]))

    seg = jnp.arange(parents.shape[0], dtype=jnp.int32)
    block = seg >> 1
    from_leaf, from_z = block >> 3, block & (NZ - 1)
    z = (from_z - ctx) & (NZ - 1)
    z = jnp.where(z == 0, 0, jnp.where(z < 4, 2 * z, jnp.where(z == 4, 7, 2 * (NZ - z) - 1)))
    x = ((from_leaf >> 1) - (leaf >> 1)) & (NX - 1)
    x = jnp.where(x == 0, 0, jnp.where(x == 1, 2, jnp.where(x == 2, 3, 1)))
    place = jnp.where((seg & 1) == 0, x * NZ + z, z * NX + x)
    place = place + NX * NZ * ((from_leaf ^ leaf) & 1)
    lists, counts = walk(parents, info, place)
    rows1, lists, counts, came[2], came[6] = lax.optimization_barrier(
        (rows1, lists, counts, came[2], came[6])
    )

    even = ring_x(cat(*ring_z(project(where, *rows0, key_weight, value_weight))))
    odd = cat(*ring_x(project(where, *rows1, key_weight, value_weight)))
    qt = unpack(table, came)
    odd, qt = lax.optimization_barrier((odd, qt))
    odd = ring_z(odd)
    odd = [odd[0]] + [cat(a, b) for a, b in zip(odd[1::2], odd[2::2])]

    def both(pieces):
        pieces = pieces + [lax.ppermute(a, "leaf", CS) for a in pieces]
        return [a.reshape(-1, 2 * SEG, 2 * HEAD) for a in pieces]

    state = attend(0, lists, counts, info, qt, both(even), None)
    return attend(1, lists, counts, info, qt, both(odd), state)


def solution(mesh):
    in_specs = (
        P(("leaf", "ctx"), "head"),
        P(("leaf", "ctx"), "head"),
        P(None, "head"),
        P(None, "head"),
        P(),
        P(),
    )
    out_specs = P(("leaf", "ctx"), "head")
    return jax.shard_map(
        on_device, mesh=mesh, in_specs=in_specs, out_specs=out_specs, check_vma=False
    )
```

```python
import functools
import math

import jax
import jax.numpy as jnp
from jax import lax
from jax.experimental import pallas as pl
from jax.experimental.pallas import tpu as pltpu
from jax.sharding import PartitionSpec as P

HEAD = 128
GROUP = 8
SEG = 128
TILE = 32
TPD = 8
CAP = 2
NX, NZ, NY = 4, 8, 4
ROWS = TILE * GROUP
SCALE = math.log2(math.e) / math.sqrt(HEAD)
FILL = -1.2e31
MIB = 1 << 20
UNIT = 4
LIST = 32 + 16
PASSES = 5

XP = [(2 * x + c, 2 * ((x + 1) % NX) + c) for x in range(NX) for c in range(2)]
XM = [(2 * x + c, 2 * ((x - 1) % NX) + c) for x in range(NX) for c in range(2)]
CS = [(i, i ^ 1) for i in range(2 * NX)]


def turn(n, by):
    return [(i, (i + by) % n) for i in range(n)]


ZP, ZM = turn(NZ, 1), turn(NZ, -1)
YP, YM = turn(NY, 1), turn(NY, -1)

smem = functools.partial(pl.BlockSpec, memory_space=pltpu.SMEM)
vmem = functools.partial(pl.BlockSpec, memory_space=pltpu.VMEM)


def pack_kernel(where, dest, q, *outs):
    sends, table, info = outs[:NZ], outs[NZ], outs[NZ + 1]
    leaf, ctx = where[0], where[1]
    device = leaf * NZ + ctx
    shifts = [((dest[device * TPD + j] >> 3) - ctx) & (NZ - 1) for j in range(TPD)]
    ranks = []
    for j in range(TPD):
        rank = jnp.int32(0)
        for i in range(j):
            rank = rank + (shifts[i] == shifts[j]).astype(jnp.int32)
        ranks.append(rank)
    for s in range(NZ):
        for r in range(CAP):
            pick = jnp.int32(0)
            for j in range(TPD):
                pick = jnp.where((shifts[j] == s) & (ranks[j] == r), j, pick)
            sends[s][r] = q[pl.ds(pl.multiple_of(pick * TILE, TILE), TILE), :]
    for s in range(NZ):
        base = (leaf * NZ + ((ctx - s) & (NZ - 1))) * TPD
        table[s * CAP] = jnp.int32(-1)
        table[s * CAP + 1] = jnp.int32(-1)

        def one(j, rank, s=s, base=base):
            to = dest[base + j]
            mine = (to >> 3) == device

            @pl.when(mine)
            def _():
                table[s * CAP + rank] = to & (TPD - 1)
                info[to & (TPD - 1)] = base + j

            return rank + mine.astype(jnp.int32)

        lax.fori_loop(0, TPD, one, jnp.int32(0))


def pack(where, dest, q):
    width = q.shape[1]
    outs = pl.pallas_call(
        pack_kernel,
        in_specs=[smem(), smem(), vmem()],
        out_specs=[vmem()] * NZ + [smem(), smem()],
        out_shape=[jax.ShapeDtypeStruct((CAP, TILE, width), q.dtype)] * NZ
        + [jax.ShapeDtypeStruct((NZ * CAP,), jnp.int32), jax.ShapeDtypeStruct((TPD,), jnp.int32)],
        compiler_params=pltpu.CompilerParams(vmem_limit_bytes=32 * MIB),
        cost_estimate=pl.CostEstimate(flops=0, bytes_accessed=3 * MIB, transcendentals=0),
        name="pack",
    )(where, dest, q)
    return outs[:NZ], outs[NZ], outs[NZ + 1]


def walk_kernel(parents, info, which, place, lists, counts):
    def tile(d, carry):
        for p in range(PASSES):
            counts[p * TPD + d] = jnp.int32(0)

        def body(at):
            row = which[at] * TPD + d
            used = counts[row]
            lists[row * LIST + used] = place[at]
            counts[row] = used + 1
            return parents[at]

        seg = info[d] >> 2
        lax.while_loop(lambda at: at >= 0, body, seg)
        counts[PASSES * TPD + d] = which[seg]
        for p in range(PASSES):
            row = p * TPD + d
            used = row * LIST + counts[row]
            for n in range(2 * UNIT):
                lists[used + n] = jnp.int32(0)
        return carry

    lax.fori_loop(0, TPD, tile, 0)


def walk(parents, info, which, place):
    return pl.pallas_call(
        walk_kernel,
        in_specs=[smem()] * 4,
        out_specs=[smem()] * 2,
        out_shape=[
            jax.ShapeDtypeStruct((PASSES * TPD * LIST,), jnp.int32),
            jax.ShapeDtypeStruct(((PASSES + 1) * TPD,), jnp.int32),
        ],
        cost_estimate=pl.CostEstimate(flops=0, bytes_accessed=16 * MIB, transcendentals=0),
        name="walk",
    )(parents, info, which, place)


def unpack_kernel(table, *refs):
    came, out = refs[:NZ], refs[NZ]
    for s in range(NZ):

        def one(r, carry, s=s):
            d = table[s * CAP + r]

            @pl.when(d >= 0)
            def _():
                for g in range(2):
                    heads = [
                        came[s][r, :, pl.ds((g * GROUP + h) * HEAD, HEAD)] for h in range(GROUP)
                    ]
                    out[d, g] = jnp.concatenate(heads, axis=0).T

            return carry

        lax.fori_loop(0, CAP, one, 0)


def unpack(table, came):
    return pl.pallas_call(
        unpack_kernel,
        in_specs=[smem()] + [vmem()] * NZ,
        out_specs=vmem(),
        out_shape=jax.ShapeDtypeStruct((TPD, 2, HEAD, ROWS), jnp.bfloat16),
        compiler_params=pltpu.CompilerParams(vmem_limit_bytes=32 * MIB),
        cost_estimate=pl.CostEstimate(flops=0, bytes_accessed=6 * MIB, transcendentals=0),
        name="unpack",
    )(table, *came)


def project_kernel(where, own, before, after, far0, far1, wk, wv, out):
    y = where[2]
    depth = own.shape[1]
    half = far0.shape[0]

    def rows(by):
        at = (y + by) & (NY - 1)
        return pl.ds(pl.multiple_of(at * depth, depth), depth)

    def times(w):
        total = jnp.dot(own[...], w[rows(0), :], preferred_element_type=jnp.float32)
        total += jnp.dot(before[...], w[rows(NY - 1), :], preferred_element_type=jnp.float32)
        total += jnp.dot(after[...], w[rows(1), :], preferred_element_type=jnp.float32)
        far = jnp.concatenate([far0[...], far1[...]], axis=0)
        return total + jnp.dot(far, w[rows(2), :], preferred_element_type=jnp.float32)

    k = times(wk)
    v = times(wv)
    for n in range(2):
        at = n * 2 * SEG
        out[at : at + SEG, :] = k[n * SEG : (n + 1) * SEG].astype(out.dtype)
        for g in range(2):
            part = v[n * SEG : (n + 1) * SEG, g * HEAD : (g + 1) * HEAD]
            out[at + SEG : at + 2 * SEG, g * HEAD : (g + 1) * HEAD] = part.T.astype(out.dtype)


def project(where, own, before, after, far0, far1, wk, wv):
    return pl.pallas_call(
        project_kernel,
        in_specs=[smem()] + [vmem()] * 7,
        out_specs=vmem(),
        out_shape=jax.ShapeDtypeStruct((4 * SEG, 2 * HEAD), jnp.bfloat16),
        compiler_params=pltpu.CompilerParams(vmem_limit_bytes=40 * MIB),
        cost_estimate=pl.CostEstimate(flops=2 * 256 * 5120 * 512, bytes_accessed=8 * MIB, transcendentals=0),
        name="project",
    )(where, own, before, after, far0, far1, wk, wv)


def attend_kernel(which, n_pieces, lists, counts, info, qt, *refs):
    pieces, refs = refs[:n_pieces], refs[n_pieces:]
    first, finish = which == 0, which == PASSES - 1
    if not first:
        old_top, old_total, old_sum, refs = *refs[:3], refs[3:]
    if finish:
        out, kv, score, peak, weight, sems, top, total, acc = refs
    else:
        top, total, acc, kv, score, peak, weight, sems = refs
    copies, at = [], 0
    for n, piece in enumerate(pieces):
        size = piece.shape[0]
        copies.append(pltpu.make_async_copy(piece, kv.at[pl.ds(at, size)], sems.at[n]))
        at += size
    for copy in copies:
        copy.start()
    for copy in copies:
        copy.wait()

    def keys(w, g):
        return kv[w, 0:SEG, g * HEAD : (g + 1) * HEAD]

    def tile(d, carry):
        base = (which * TPD + d) * LIST
        count = counts[which * TPD + d]
        ids = [d * 2 + g for g in range(2)]

        def spots(i):
            return [lists[base + i * UNIT + u] for u in range(UNIT)]

        def scores(places, limit=None):
            for g in range(2):
                k = jnp.concatenate([keys(w, g) for w in places], axis=0)
                s = jnp.dot(k, qt[d, g], preferred_element_type=jnp.float32)
                if limit is not None:
                    key = lax.broadcasted_iota(jnp.int32, (UNIT * SEG, ROWS), 0)
                    s = jnp.where((key <= limit) | (key >= SEG), s, FILL)
                score[g] = s
                for u in range(UNIT):
                    part = s[u * SEG : (u + 1) * SEG].reshape(SEG // 8, 8, ROWS)
                    peak[g, u] = jnp.max(part, axis=0)

        for g in range(2):
            i = ids[g]
            if not first:
                top[i], total[i], acc[i] = old_top[i], old_total[i], old_sum[i]
            else:
                top[i] = jnp.full((1, ROWS), FILL, jnp.float32)
                total[i] = jnp.zeros((1, ROWS), jnp.float32)
                acc[i] = jnp.zeros((HEAD, ROWS), jnp.float32)
            weight[g] = jnp.zeros_like(weight[g])
        own, quarter = counts[PASSES * TPD + d] == which, info[d] & 3
        token = lax.broadcasted_iota(jnp.int32, (UNIT * SEG, ROWS), 1) & (TILE - 1)
        scores(spots(0), token + jnp.where(own, quarter * TILE, SEG))
        def add(places, drops):
            for g in range(2):
                v = jnp.concatenate(
                    [kv[w, SEG : 2 * SEG, g * HEAD : (g + 1) * HEAD] for w in places], axis=1
                )
                acc[ids[g]] = acc[ids[g]] * drops[g] + jnp.dot(
                    v, weight[g], preferred_element_type=jnp.float32
                )

        def body(i, drops):
            later = spots(i + 1)
            pens = [jnp.where(i * UNIT + u < count, 0.0, 3e31) for u in range(UNIT)]
            result = []
            add(spots(jnp.maximum(i - 1, 0)), drops)
            for g in range(2):
                old = top[ids[g]]
                peaks = [
                    peak[g, u] - pens[u] for u in range(UNIT)
                ]
                peaks = jnp.max(functools.reduce(jnp.maximum, peaks), axis=0, keepdims=True)
                new = jnp.maximum(old, peaks)
                drop = jnp.exp2((old - new) * SCALE)
                part = jnp.zeros((8, ROWS), jnp.float32)
                for u in range(UNIT):
                    e = jnp.exp2((score[g, u * SEG : (u + 1) * SEG] - (new + pens[u])) * SCALE)
                    part += jnp.sum(e.reshape(SEG // 8, 8, ROWS), axis=0)
                    weight[g, u * SEG : (u + 1) * SEG] = e.astype(jnp.bfloat16)
                total[ids[g]] = total[ids[g]] * drop + jnp.sum(part, axis=0, keepdims=True)
                top[ids[g]] = new
                result.append(drop)
            scores(later)
            return tuple(result)

        rounds = (count + UNIT - 1) // UNIT
        ones = jnp.ones((1, ROWS), jnp.float32)
        drops = lax.fori_loop(0, rounds, body, (ones, ones))
        add(spots(jnp.maximum(rounds - 1, 0)), drops)

        if finish:
            for g in range(2):
                i = ids[g]
                o = (acc[i] / total[i]).T.astype(out.dtype)
                for h in range(GROUP):
                    out[
                        pl.ds(pl.multiple_of(d * TILE, TILE), TILE),
                        (g * GROUP + h) * HEAD : (g * GROUP + h + 1) * HEAD,
                    ] = o[h * TILE : (h + 1) * TILE]
        return carry

    lax.fori_loop(0, TPD, tile, 0)


def attend(which, lists, counts, info, qt, pieces, state):
    first, finish = which == 0, which == PASSES - 1
    shapes = [
        jax.ShapeDtypeStruct((2 * TPD, 1, ROWS), jnp.float32),
        jax.ShapeDtypeStruct((2 * TPD, 1, ROWS), jnp.float32),
        jax.ShapeDtypeStruct((2 * TPD, HEAD, ROWS), jnp.float32),
    ]
    result = jax.ShapeDtypeStruct((TPD * TILE, 2 * GROUP * HEAD), jnp.bfloat16)
    blocks = sum(piece.shape[0] for piece in pieces)
    scratch = [
        pltpu.VMEM((blocks, 2 * SEG, 2 * HEAD), jnp.bfloat16),
        pltpu.VMEM((2, UNIT * SEG, ROWS), jnp.float32),
        pltpu.VMEM((2, UNIT, 8, ROWS), jnp.float32),
        pltpu.VMEM((2, UNIT * SEG, ROWS), jnp.bfloat16),
        pltpu.SemaphoreType.DMA((len(pieces),)),
    ]
    if finish:
        scratch += [pltpu.VMEM(a.shape, a.dtype) for a in shapes]
    return pl.pallas_call(
        functools.partial(attend_kernel, which, len(pieces)),
        in_specs=[smem()] * 3
        + [vmem()]
        + [pl.BlockSpec(memory_space=pl.ANY)] * len(pieces)
        + [vmem()] * (0 if first else 3),
        out_specs=vmem() if finish else [vmem()] * 3,
        out_shape=result if finish else shapes,
        scratch_shapes=scratch,
        compiler_params=pltpu.CompilerParams(vmem_limit_bytes=28 * MIB),
        cost_estimate=pl.CostEstimate(
            flops=256 * 16 * 128 * 128 * 32, bytes_accessed=6 * MIB, transcendentals=0
        ),
        name="attend",
    )(lists, counts, info, qt, *pieces, *(() if first else state))


def cat(*parts):
    return jnp.concatenate(parts, axis=0)


def ring_four(block, axis, up, down, ready=()):
    half = block.shape[0] // 2
    low = lax.ppermute(block, axis, up)
    high = lax.ppermute(block, axis, down)
    low, high, _ = lax.optimization_barrier((low, high, ready))
    far0 = lax.ppermute(low[:half], axis, up)
    far1 = lax.ppermute(high[half:], axis, down)
    return [block, low, high, far0, far1]


def swapped(pieces):
    pieces = pieces + [lax.ppermute(a, "leaf", CS) for a in pieces]
    return [a.reshape(-1, 2 * SEG, 2 * HEAD) for a in pieces]


def on_device(queries, inputs, key_weight, value_weight, parents, tile_dest):
    leaf, ctx, y = lax.axis_index("leaf"), lax.axis_index("ctx"), lax.axis_index("head")
    where = jnp.stack([leaf, ctx, y]).astype(jnp.int32)
    sends, table, info = pack(where, tile_dest, queries)
    came = [sends[0]] + [lax.ppermute(sends[s], "ctx", turn(NZ, s)) for s in range(1, NZ)]
    rows = ring_four(inputs, "head", YP, YM, sends)

    seg = jnp.arange(parents.shape[0], dtype=jnp.int32)
    block = seg >> 1
    from_leaf, from_z = block >> 3, block & (NZ - 1)
    z = (from_z - ctx) & (NZ - 1)
    x = ((from_leaf >> 1) - (leaf >> 1)) & (NX - 1)
    x = jnp.where(x == 0, 0, jnp.where(x == 1, 2, jnp.where(x == 2, 3, 1)))
    which = jnp.where(z <= 4, z, NZ - z)
    side = jnp.where((which == 0) | (which == 4), 0, jnp.where(z < 4, 1, 0))
    span = jnp.where((which == 0) | (which == 4), 8, 16)
    place = x * 2 + (seg & 1) + side * 8 + span * ((from_leaf ^ leaf) & 1)
    lists, counts = walk(parents, info, which, place)
    rows, lists, counts = lax.optimization_barrier((rows, lists, counts))

    plane = cat(*ring_four(project(where, *rows, key_weight, value_weight), "leaf", XP, XM))
    qt = unpack(table, came)
    plane, qt = lax.optimization_barrier((plane, qt))

    low = high = plane
    pieces, state = [plane], None
    for p in range(PASSES - 1):
        half = plane.shape[0] // 2
        if p < PASSES - 2:
            low, high = lax.ppermute(low, "ctx", ZP), lax.ppermute(high, "ctx", ZM)
        else:
            low, high = lax.ppermute(low[:half], "ctx", ZP), lax.ppermute(high[half:], "ctx", ZM)
        state = attend(p, lists, counts, info, qt, swapped(pieces), state)
        low, high, state = lax.optimization_barrier((low, high, state))
        pieces = [low, high]
    return attend(PASSES - 1, lists, counts, info, qt, swapped(pieces), state)


def solution(mesh):
    in_specs = (
        P(("leaf", "ctx"), "head"),
        P(("leaf", "ctx"), "head"),
        P(None, "head"),
        P(None, "head"),
        P(),
        P(),
    )
    out_specs = P(("leaf", "ctx"), "head")
    return jax.shard_map(
        on_device, mesh=mesh, in_specs=in_specs, out_specs=out_specs, check_vma=False
    )
```

```python
import functools
import math

import jax
import jax.numpy as jnp
from jax import lax
from jax.experimental import pallas as pl
from jax.experimental.pallas import tpu as pltpu
from jax.sharding import PartitionSpec as P

HEAD = 128
GROUP = 8
SEG = 128
TILE = 32
TPD = 8
CAP = 2
NX, NZ, NY = 4, 8, 4
ROWS = TILE * GROUP
SCALE = math.log2(math.e) / math.sqrt(HEAD)
FILL = -1.2e31
MIB = 1 << 20
UNIT = 4
PASSES = 5
ITEMS = 8 * 32 // UNIT + 4

XP = [(2 * x + c, 2 * ((x + 1) % NX) + c) for x in range(NX) for c in range(2)]
XM = [(2 * x + c, 2 * ((x - 1) % NX) + c) for x in range(NX) for c in range(2)]
CS = [(i, i ^ 1) for i in range(2 * NX)]


def turn(n, by):
    return [(i, (i + by) % n) for i in range(n)]


ZP, ZM = turn(NZ, 1), turn(NZ, -1)
YP, YM = turn(NY, 1), turn(NY, -1)

smem = functools.partial(pl.BlockSpec, memory_space=pltpu.SMEM)
vmem = functools.partial(pl.BlockSpec, memory_space=pltpu.VMEM)


def pack_kernel(where, dest, q, *outs):
    sends, table, info = outs[:NZ], outs[NZ], outs[NZ + 1]
    leaf, ctx = where[0], where[1]
    device = leaf * NZ + ctx
    shifts = [((dest[device * TPD + j] >> 3) - ctx) & (NZ - 1) for j in range(TPD)]
    ranks = []
    for j in range(TPD):
        rank = jnp.int32(0)
        for i in range(j):
            rank = rank + (shifts[i] == shifts[j]).astype(jnp.int32)
        ranks.append(rank)
    for s in range(NZ):
        for r in range(CAP):
            pick = jnp.int32(0)
            for j in range(TPD):
                pick = jnp.where((shifts[j] == s) & (ranks[j] == r), j, pick)
            sends[s][r] = q[pl.ds(pl.multiple_of(pick * TILE, TILE), TILE), :]
    for s in range(NZ):
        base = (leaf * NZ + ((ctx - s) & (NZ - 1))) * TPD
        table[s * CAP] = jnp.int32(-1)
        table[s * CAP + 1] = jnp.int32(-1)

        def one(j, rank, s=s, base=base):
            to = dest[base + j]
            mine = (to >> 3) == device

            @pl.when(mine)
            def _():
                table[s * CAP + rank] = to & (TPD - 1)
                info[to & (TPD - 1)] = base + j

            return rank + mine.astype(jnp.int32)

        lax.fori_loop(0, TPD, one, jnp.int32(0))


def pack(where, dest, q):
    width = q.shape[1]
    outs = pl.pallas_call(
        pack_kernel,
        in_specs=[smem(), smem(), vmem()],
        out_specs=[vmem()] * NZ + [smem(), smem()],
        out_shape=[jax.ShapeDtypeStruct((CAP, TILE, width), q.dtype)] * NZ
        + [jax.ShapeDtypeStruct((NZ * CAP,), jnp.int32), jax.ShapeDtypeStruct((TPD,), jnp.int32)],
        compiler_params=pltpu.CompilerParams(vmem_limit_bytes=32 * MIB),
        cost_estimate=pl.CostEstimate(flops=0, bytes_accessed=3 * MIB, transcendentals=0),
        name="pack",
    )(where, dest, q)
    return outs[:NZ], outs[NZ], outs[NZ + 1]


def walk_kernel(parents, info, which, place, lists, tiles, counts):
    for p in range(PASSES):
        counts[p] = jnp.int32(0)

    def tile(d, carry):
        seg = info[d] >> 2

        def body(at):
            p = which[at]
            used = counts[p]

            @pl.when((used & (UNIT - 1)) == 0)
            def _():
                tiles[p * ITEMS + used // UNIT] = d + jnp.where(at == seg, TPD, 0)

            lists[p * ITEMS * UNIT + used] = place[at]
            counts[p] = used + 1
            return parents[at]

        lax.while_loop(lambda at: at >= 0, body, seg)
        for p in range(PASSES):
            used = counts[p]
            for n in range(UNIT):
                lists[p * ITEMS * UNIT + used + n] = jnp.int32(-1)
            counts[p] = ((used + UNIT - 1) // UNIT) * UNIT
        return carry

    lax.fori_loop(0, TPD, tile, 0)
    for p in range(PASSES):
        used = counts[p]
        tiles[p * ITEMS + used // UNIT] = jnp.int32(0)
        for n in range(UNIT):
            lists[p * ITEMS * UNIT + used + n] = jnp.int32(-1)


def walk(parents, info, which, place):
    return pl.pallas_call(
        walk_kernel,
        in_specs=[smem()] * 4,
        out_specs=[smem()] * 3,
        out_shape=[
            jax.ShapeDtypeStruct((PASSES * ITEMS * UNIT,), jnp.int32),
            jax.ShapeDtypeStruct((PASSES * ITEMS,), jnp.int32),
            jax.ShapeDtypeStruct((PASSES,), jnp.int32),
        ],
        cost_estimate=pl.CostEstimate(flops=0, bytes_accessed=16 * MIB, transcendentals=0),
        name="walk",
    )(parents, info, which, place)


def unpack_kernel(table, *refs):
    came, out = refs[:NZ], refs[NZ]
    for s in range(NZ):

        def one(r, carry, s=s):
            d = table[s * CAP + r]

            @pl.when(d >= 0)
            def _():
                for g in range(2):
                    heads = [
                        came[s][r, :, pl.ds((g * GROUP + h) * HEAD, HEAD)] for h in range(GROUP)
                    ]
                    out[d, g] = jnp.concatenate(heads, axis=0).T

            return carry

        lax.fori_loop(0, CAP, one, 0)


def unpack(table, came):
    return pl.pallas_call(
        unpack_kernel,
        in_specs=[smem()] + [vmem()] * NZ,
        out_specs=vmem(),
        out_shape=jax.ShapeDtypeStruct((TPD, 2, HEAD, ROWS), jnp.bfloat16),
        compiler_params=pltpu.CompilerParams(vmem_limit_bytes=32 * MIB),
        cost_estimate=pl.CostEstimate(flops=0, bytes_accessed=6 * MIB, transcendentals=0),
        name="unpack",
    )(table, *came)


def project_kernel(where, own, before, after, far0, far1, wk, wv, out):
    y = where[2]
    depth = own.shape[1]
    half = far0.shape[0]

    def rows(by):
        at = (y + by) & (NY - 1)
        return pl.ds(pl.multiple_of(at * depth, depth), depth)

    def times(w):
        total = jnp.dot(own[...], w[rows(0), :], preferred_element_type=jnp.float32)
        total += jnp.dot(before[...], w[rows(NY - 1), :], preferred_element_type=jnp.float32)
        total += jnp.dot(after[...], w[rows(1), :], preferred_element_type=jnp.float32)
        far = jnp.concatenate([far0[...], far1[...]], axis=0)
        return total + jnp.dot(far, w[rows(2), :], preferred_element_type=jnp.float32)

    k = times(wk)
    v = times(wv)
    for n in range(2):
        at = n * 2 * SEG
        out[at : at + SEG, :] = k[n * SEG : (n + 1) * SEG].astype(out.dtype)
        for g in range(2):
            part = v[n * SEG : (n + 1) * SEG, g * HEAD : (g + 1) * HEAD]
            out[at + SEG : at + 2 * SEG, g * HEAD : (g + 1) * HEAD] = part.T.astype(out.dtype)


def project(where, own, before, after, far0, far1, wk, wv):
    return pl.pallas_call(
        project_kernel,
        in_specs=[smem()] + [vmem()] * 7,
        out_specs=vmem(),
        out_shape=jax.ShapeDtypeStruct((4 * SEG, 2 * HEAD), jnp.bfloat16),
        compiler_params=pltpu.CompilerParams(vmem_limit_bytes=40 * MIB),
        cost_estimate=pl.CostEstimate(flops=2 * 256 * 5120 * 512, bytes_accessed=8 * MIB, transcendentals=0),
        name="project",
    )(where, own, before, after, far0, far1, wk, wv)


def attend_kernel(which, n_pieces, lists, tiles, counts, info, qt, *refs):
    pieces, refs = refs[:n_pieces], refs[n_pieces:]
    first, finish = which == 0, which == PASSES - 1
    if not first:
        refs = refs[3:]
    top, total, acc = refs[:3]
    if finish:
        out, kv, score, peak, weight, sems = refs[3:]
    else:
        kv, score, peak, weight, sems = refs[3:]
    copies, at = [], 0
    for n, piece in enumerate(pieces):
        size = piece.shape[0]
        copies.append(pltpu.make_async_copy(piece, kv.at[pl.ds(at, size)], sems.at[n]))
        at += size
    for copy in copies:
        copy.start()
    if first:
        top[...] = jnp.full(top.shape, FILL, jnp.float32)
        total[...] = jnp.zeros(total.shape, jnp.float32)
        acc[...] = jnp.zeros(acc.shape, jnp.float32)
    weight[...] = jnp.zeros(weight.shape, weight.dtype)
    for copy in copies:
        copy.wait()

    def entries(j):
        return [lists[(which * ITEMS + j) * UNIT + u] for u in range(UNIT)]

    def places(j):
        return [jnp.maximum(e, 0) for e in entries(j)]

    def tile_of(j):
        return tiles[which * ITEMS + j] & (TPD - 1)

    def scores(j):
        d, spots = tile_of(j), places(j)
        for g in range(2):
            k = jnp.concatenate([kv[w, 0:SEG, g * HEAD : (g + 1) * HEAD] for w in spots], axis=0)
            s = jnp.dot(k, qt[d, g], preferred_element_type=jnp.float32)
            score[g] = s
            for u in range(UNIT):
                part = s[u * SEG : (u + 1) * SEG].reshape(SEG // 8, 8, ROWS)
                peak[g, u] = jnp.max(part, axis=0)

        @pl.when(tiles[which * ITEMS + j] >= TPD)
        def _():
            key = lax.broadcasted_iota(jnp.int32, (SEG, ROWS), 0)
            token = lax.broadcasted_iota(jnp.int32, (SEG, ROWS), 1) & (TILE - 1)
            ok = key <= token + (info[d] & 3) * TILE
            for g in range(2):
                s = jnp.where(ok, score[g, 0:SEG], FILL)
                score[g, 0:SEG] = s
                peak[g, 0] = jnp.max(s.reshape(SEG // 8, 8, ROWS), axis=0)

    def add(j, drops):
        d, spots = tile_of(j), places(j)
        for g in range(2):
            v = jnp.concatenate(
                [kv[w, SEG : 2 * SEG, g * HEAD : (g + 1) * HEAD] for w in spots], axis=1
            )
            acc[d * 2 + g] = acc[d * 2 + g] * drops[g] + jnp.dot(
                v, weight[g], preferred_element_type=jnp.float32
            )

    def body(j, drops):
        add(jnp.maximum(j - 1, 0), drops)
        d = tile_of(j)
        pens = [jnp.where(e < 0, 3e31, 0.0) for e in entries(j)]
        result = []
        for g in range(2):
            i = d * 2 + g
            old = top[i]
            peaks = functools.reduce(jnp.maximum, [peak[g, u] - pens[u] for u in range(UNIT)])
            new = jnp.maximum(old, jnp.max(peaks, axis=0, keepdims=True))
            drop = jnp.exp2((old - new) * SCALE)
            part = jnp.zeros((8, ROWS), jnp.float32)
            for u in range(UNIT):
                e = jnp.exp2((score[g, u * SEG : (u + 1) * SEG] - (new + pens[u])) * SCALE)
                part += jnp.sum(e.reshape(SEG // 8, 8, ROWS), axis=0)
                weight[g, u * SEG : (u + 1) * SEG] = e.astype(jnp.bfloat16)
            total[i] = total[i] * drop + jnp.sum(part, axis=0, keepdims=True)
            top[i] = new
            result.append(drop)
        scores(j + 1)
        return tuple(result)

    rounds = counts[which] // UNIT
    ones = jnp.ones((1, ROWS), jnp.float32)
    scores(0)
    drops = lax.fori_loop(0, rounds, body, (ones, ones))
    add(jnp.maximum(rounds - 1, 0), drops)

    if finish:

        def write(d, carry):
            for g in range(2):
                i = d * 2 + g
                o = (acc[i] / total[i]).T.astype(out.dtype)
                for h in range(GROUP):
                    out[
                        pl.ds(pl.multiple_of(d * TILE, TILE), TILE),
                        (g * GROUP + h) * HEAD : (g * GROUP + h + 1) * HEAD,
                    ] = o[h * TILE : (h + 1) * TILE]
            return carry

        lax.fori_loop(0, TPD, write, 0)


def attend(which, work, qt, pieces, state):
    first, finish = which == 0, which == PASSES - 1
    shapes = [
        jax.ShapeDtypeStruct((2 * TPD, 1, ROWS), jnp.float32),
        jax.ShapeDtypeStruct((2 * TPD, 1, ROWS), jnp.float32),
        jax.ShapeDtypeStruct((2 * TPD, HEAD, ROWS), jnp.float32),
    ]
    if finish:
        shapes.append(jax.ShapeDtypeStruct((TPD * TILE, 2 * GROUP * HEAD), jnp.bfloat16))
    blocks = sum(piece.shape[0] for piece in pieces)
    begin = len(work) + 1 + len(pieces)
    return pl.pallas_call(
        functools.partial(attend_kernel, which, len(pieces)),
        in_specs=[smem()] * len(work)
        + [vmem()]
        + [pl.BlockSpec(memory_space=pl.ANY)] * len(pieces)
        + [vmem()] * (0 if first else 3),
        out_specs=[vmem()] * len(shapes),
        out_shape=shapes,
        input_output_aliases={} if first else {begin + n: n for n in range(3)},
        scratch_shapes=[
            pltpu.VMEM((blocks, 2 * SEG, 2 * HEAD), jnp.bfloat16),
            pltpu.VMEM((2, UNIT * SEG, ROWS), jnp.float32),
            pltpu.VMEM((2, UNIT, 8, ROWS), jnp.float32),
            pltpu.VMEM((2, UNIT * SEG, ROWS), jnp.bfloat16),
            pltpu.SemaphoreType.DMA((len(pieces),)),
        ],
        compiler_params=pltpu.CompilerParams(vmem_limit_bytes=28 * MIB),
        cost_estimate=pl.CostEstimate(
            flops=256 * 16 * 128 * 128 * 32, bytes_accessed=6 * MIB, transcendentals=0
        ),
        name="attend",
    )(*work, qt, *pieces, *(() if first else state))


def cat(*parts):
    return jnp.concatenate(parts, axis=0)


def ring_four(block, axis, up, down, ready=()):
    half = block.shape[0] // 2
    low = lax.ppermute(block, axis, up)
    high = lax.ppermute(block, axis, down)
    low, high, _ = lax.optimization_barrier((low, high, ready))
    far0 = lax.ppermute(low[:half], axis, up)
    far1 = lax.ppermute(high[half:], axis, down)
    return [block, low, high, far0, far1]


def ring_z(block):
    half = block.shape[0] // 2
    parts = [block]
    low = high = block
    for _ in range(3):
        low = lax.ppermute(low, "ctx", ZP)
        high = lax.ppermute(high, "ctx", ZM)
        parts += [low, high]
    return parts + [lax.ppermute(low[:half], "ctx", ZP), lax.ppermute(high[half:], "ctx", ZM)]


def swapped(*pieces):
    pieces = list(pieces) + [lax.ppermute(a, "leaf", CS) for a in pieces]
    return [a.reshape(-1, 2 * SEG, 2 * HEAD) for a in pieces]


def on_device(queries, inputs, key_weight, value_weight, parents, tile_dest):
    leaf, ctx, y = lax.axis_index("leaf"), lax.axis_index("ctx"), lax.axis_index("head")
    where = jnp.stack([leaf, ctx, y]).astype(jnp.int32)
    sends, table, info = pack(where, tile_dest, queries)
    came = [sends[0]] + [lax.ppermute(sends[s], "ctx", turn(NZ, s)) for s in range(1, NZ)]
    rows = ring_four(inputs, "head", YP, YM, sends)

    seg = jnp.arange(parents.shape[0], dtype=jnp.int32)
    odd = (seg & 1) == 1
    block = seg >> 1
    from_leaf, from_z = block >> 3, block & (NZ - 1)
    z = (from_z - ctx) & (NZ - 1)
    x = ((from_leaf >> 1) - (leaf >> 1)) & (NX - 1)
    at_z = jnp.where(z == 0, 0, jnp.where(z < 4, 2 * z, jnp.where(z == 4, 7, 2 * (NZ - z) - 1)))
    at_x = jnp.where(x == 0, 0, jnp.where(x == 1, 2, jnp.where(x == 2, 3, 1)))
    which = jnp.where(
        odd,
        jnp.where(z <= 4, z, NZ - z),
        jnp.where(x == 0, 0, jnp.where(x == 3, 2, jnp.where(x == 1, 3, 4))),
    )
    ahead = jnp.where(odd & (z > 0) & (z < 4), 4, 0)
    start_odd = jnp.where(which == 0, 8, ahead)
    start_even = jnp.where(which == 0, 0, jnp.where(which == 4, 4, 8))
    place = jnp.where(odd, start_odd + at_x, start_even + at_z)
    span = jnp.where((which == 0) | (which == 4), 12, jnp.where(which == 1, 8, 16))
    place = place + span * ((from_leaf ^ leaf) & 1)
    work = list(walk(parents, info, which, place))
    rows, work, early = lax.optimization_barrier((rows, work, came[1:4] + came[5:]))
    came = [came[0]] + early[:3] + [came[4]] + early[3:]
    work.append(info)

    kv = project(where, *rows, key_weight, value_weight)
    half = kv.shape[0] // 2
    odds = cat(*ring_four(kv[half:], "leaf", XP, XM))
    evens = cat(*ring_z(kv[:half]))
    qt = unpack(table, came)
    odds, evens, qt = lax.optimization_barrier((odds, evens, qt))

    def along_z(a, b):
        return lax.ppermute(a, "ctx", ZP), lax.ppermute(b, "ctx", ZM)

    low, high = along_z(odds, odds)
    low_x, high_x = lax.ppermute(evens, "leaf", XP), lax.ppermute(evens, "leaf", XM)
    state = attend(0, work, qt, swapped(evens, odds), None)
    low, high, state = lax.optimization_barrier((low, high, state))
    pieces = swapped(low, high)
    low, high = along_z(low, high)
    state = attend(1, work, qt, pieces, state)
    low, high, low_x, high_x, state = lax.optimization_barrier((low, high, low_x, high_x, state))
    pieces = swapped(low, high, low_x)
    low, high = along_z(low, high)
    mid = low_x.shape[0] // 2
    far0 = lax.ppermute(low_x[:mid], "leaf", XP)
    far1 = lax.ppermute(high_x[mid:], "leaf", XM)
    state = attend(2, work, qt, pieces, state)
    low, high, high_x, state = lax.optimization_barrier((low, high, high_x, state))
    pieces = swapped(low, high, high_x)
    mid = low.shape[0] // 2
    low, high = along_z(low[:mid], high[mid:])
    state = attend(3, work, qt, pieces, state)
    low, high, far0, far1, state = lax.optimization_barrier((low, high, far0, far1, state))
    return attend(4, work, qt, swapped(low, high, far0, far1), state)[3]


def solution(mesh):
    in_specs = (
        P(("leaf", "ctx"), "head"),
        P(("leaf", "ctx"), "head"),
        P(None, "head"),
        P(None, "head"),
        P(),
        P(),
    )
    out_specs = P(("leaf", "ctx"), "head")
    return jax.shard_map(
        on_device, mesh=mesh, in_specs=in_specs, out_specs=out_specs, check_vma=False
    )
```

```python
import functools
import math

import jax
import jax.numpy as jnp
from jax import lax
from jax.experimental import pallas as pl
from jax.experimental.pallas import tpu as pltpu
from jax.sharding import PartitionSpec as P

HEAD = 128
GROUP = 8
SEG = 128
TILE = 32
TPD = 8
CAP = 2
NX, NZ, NY = 4, 8, 4
ROWS = TILE * GROUP
SCALE = math.log2(math.e) / math.sqrt(HEAD)
FILL = -1.2e31
MIB = 1 << 20
UNIT = 4
PASSES = 5
ITEMS = 8 * 32 // UNIT + 4

XP = [(2 * x + c, 2 * ((x + 1) % NX) + c) for x in range(NX) for c in range(2)]
XM = [(2 * x + c, 2 * ((x - 1) % NX) + c) for x in range(NX) for c in range(2)]
CS = [(i, i ^ 1) for i in range(2 * NX)]


def turn(n, by):
    return [(i, (i + by) % n) for i in range(n)]


ZP, ZM = turn(NZ, 1), turn(NZ, -1)
YP, YM = turn(NY, 1), turn(NY, -1)

smem = functools.partial(pl.BlockSpec, memory_space=pltpu.SMEM)
vmem = functools.partial(pl.BlockSpec, memory_space=pltpu.VMEM)


def pack_kernel(where, dest, q, *outs):
    sends, table, info = outs[:NZ], outs[NZ], outs[NZ + 1]
    leaf, ctx = where[0], where[1]
    device = leaf * NZ + ctx
    shifts = [((dest[device * TPD + j] >> 3) - ctx) & (NZ - 1) for j in range(TPD)]
    ranks = []
    for j in range(TPD):
        rank = jnp.int32(0)
        for i in range(j):
            rank = rank + (shifts[i] == shifts[j]).astype(jnp.int32)
        ranks.append(rank)
    for s in range(NZ):
        for r in range(CAP):
            pick = jnp.int32(0)
            for j in range(TPD):
                pick = jnp.where((shifts[j] == s) & (ranks[j] == r), j, pick)
            sends[s][r] = q[pl.ds(pl.multiple_of(pick * TILE, TILE), TILE), :]
    for s in range(NZ):
        base = (leaf * NZ + ((ctx - s) & (NZ - 1))) * TPD
        table[s * CAP] = jnp.int32(-1)
        table[s * CAP + 1] = jnp.int32(-1)

        def one(j, rank, s=s, base=base):
            to = dest[base + j]
            mine = (to >> 3) == device

            @pl.when(mine)
            def _():
                table[s * CAP + rank] = to & (TPD - 1)
                info[to & (TPD - 1)] = base + j

            return rank + mine.astype(jnp.int32)

        lax.fori_loop(0, TPD, one, jnp.int32(0))


def pack(where, dest, q):
    width = q.shape[1]
    outs = pl.pallas_call(
        pack_kernel,
        in_specs=[smem(), smem(), vmem()],
        out_specs=[vmem()] * NZ + [smem(), smem()],
        out_shape=[jax.ShapeDtypeStruct((CAP, TILE, width), q.dtype)] * NZ
        + [jax.ShapeDtypeStruct((NZ * CAP,), jnp.int32), jax.ShapeDtypeStruct((TPD,), jnp.int32)],
        compiler_params=pltpu.CompilerParams(vmem_limit_bytes=32 * MIB),
        cost_estimate=pl.CostEstimate(flops=0, bytes_accessed=3 * MIB, transcendentals=0),
        name="pack",
    )(where, dest, q)
    return outs[:NZ], outs[NZ], outs[NZ + 1]


def walk_kernel(parents, info, which, place, lists, tiles, counts):
    for p in range(PASSES):
        counts[p] = jnp.int32(0)

    def tile(d, carry):
        seg = info[d] >> 2

        def body(at):
            p = which[at]
            used = counts[p]

            @pl.when((used & (UNIT - 1)) == 0)
            def _():
                tiles[p * ITEMS + used // UNIT] = d + jnp.where(at == seg, TPD, 0)

            lists[p * ITEMS * UNIT + used] = place[at]
            counts[p] = used + 1
            return parents[at]

        lax.while_loop(lambda at: at >= 0, body, seg)
        for p in range(PASSES):
            used = counts[p]
            for n in range(UNIT):
                lists[p * ITEMS * UNIT + used + n] = jnp.int32(-1)
            counts[p] = ((used + UNIT - 1) // UNIT) * UNIT
        return carry

    lax.fori_loop(0, TPD, tile, 0)
    for p in range(PASSES):
        used = counts[p]
        tiles[p * ITEMS + used // UNIT] = jnp.int32(0)
        for n in range(UNIT):
            lists[p * ITEMS * UNIT + used + n] = jnp.int32(-1)


def walk(parents, info, which, place):
    return pl.pallas_call(
        walk_kernel,
        in_specs=[smem()] * 4,
        out_specs=[smem()] * 3,
        out_shape=[
            jax.ShapeDtypeStruct((PASSES * ITEMS * UNIT,), jnp.int32),
            jax.ShapeDtypeStruct((PASSES * ITEMS,), jnp.int32),
            jax.ShapeDtypeStruct((PASSES,), jnp.int32),
        ],
        cost_estimate=pl.CostEstimate(flops=0, bytes_accessed=16 * MIB, transcendentals=0),
        name="walk",
    )(parents, info, which, place)


def unpack_kernel(table, *refs):
    came, out = refs[:NZ], refs[NZ]
    for s in range(NZ):

        def one(r, carry, s=s):
            d = table[s * CAP + r]

            @pl.when(d >= 0)
            def _():
                for g in range(2):
                    heads = [
                        came[s][r, :, pl.ds((g * GROUP + h) * HEAD, HEAD)] for h in range(GROUP)
                    ]
                    out[d, g] = jnp.concatenate(heads, axis=0).T

            return carry

        lax.fori_loop(0, CAP, one, 0)


def unpack(table, came):
    return pl.pallas_call(
        unpack_kernel,
        in_specs=[smem()] + [vmem()] * NZ,
        out_specs=vmem(),
        out_shape=jax.ShapeDtypeStruct((TPD, 2, HEAD, ROWS), jnp.bfloat16),
        compiler_params=pltpu.CompilerParams(vmem_limit_bytes=32 * MIB),
        cost_estimate=pl.CostEstimate(flops=0, bytes_accessed=6 * MIB, transcendentals=0),
        name="unpack",
    )(table, *came)


def project_kernel(where, own, before, after, far0, far1, wk_hbm, wv_hbm, out, wk, wv, sems):
    y = where[2]
    depth = own.shape[1]
    order = (0, NY - 1, 1, 2)

    def rows(by):
        at = (y + by) & (NY - 1)
        return pl.ds(pl.multiple_of(at * depth, depth), depth)

    copies = []
    for n, by in enumerate(order):
        for m, (source, target) in enumerate(((wk_hbm, wk), (wv_hbm, wv))):
            copy = pltpu.make_async_copy(source.at[rows(by)], target.at[n], sems.at[n, m])
            copy.start()
            copies.append(copy)
    far = jnp.concatenate([far0[...], far1[...]], axis=0)
    k = v = 0.0
    for n, part in enumerate((own[...], before[...], after[...], far)):
        copies[2 * n].wait()
        k += jnp.dot(part, wk[n], preferred_element_type=jnp.float32)
        copies[2 * n + 1].wait()
        v += jnp.dot(part, wv[n], preferred_element_type=jnp.float32)
    for n in range(2):
        at = n * 2 * SEG
        out[at : at + SEG, :] = k[n * SEG : (n + 1) * SEG].astype(out.dtype)
        for g in range(2):
            part = v[n * SEG : (n + 1) * SEG, g * HEAD : (g + 1) * HEAD]
            out[at + SEG : at + 2 * SEG, g * HEAD : (g + 1) * HEAD] = part.T.astype(out.dtype)


def project(where, own, before, after, far0, far1, wk, wv):
    return pl.pallas_call(
        project_kernel,
        in_specs=[smem()] + [vmem()] * 5 + [pl.BlockSpec(memory_space=pl.ANY)] * 2,
        out_specs=vmem(),
        out_shape=jax.ShapeDtypeStruct((4 * SEG, 2 * HEAD), jnp.bfloat16),
        scratch_shapes=[
            pltpu.VMEM((NY, own.shape[1], wk.shape[1]), wk.dtype),
            pltpu.VMEM((NY, own.shape[1], wv.shape[1]), wv.dtype),
            pltpu.SemaphoreType.DMA((NY, 2)),
        ],
        compiler_params=pltpu.CompilerParams(vmem_limit_bytes=40 * MIB),
        cost_estimate=pl.CostEstimate(flops=2 * 256 * 5120 * 512, bytes_accessed=8 * MIB, transcendentals=0),
        name="project",
    )(where, own, before, after, far0, far1, wk, wv)


def attend_kernel(which, n_pieces, lists, tiles, counts, info, qt, *refs):
    pieces, refs = refs[:n_pieces], refs[n_pieces:]
    first, finish = which == 0, which == PASSES - 1
    if not first:
        refs = refs[3:]
    top, total, acc = refs[:3]
    if finish:
        out, kv, score, peak, weight, sems = refs[3:]
    else:
        kv, score, peak, weight, sems = refs[3:]
    copies, at = [], 0
    for n, piece in enumerate(pieces):
        size = piece.shape[0]
        copies.append(pltpu.make_async_copy(piece, kv.at[pl.ds(at, size)], sems.at[n]))
        at += size
    for copy in copies:
        copy.start()
    if first:
        top[...] = jnp.full(top.shape, FILL, jnp.float32)
        total[...] = jnp.zeros(total.shape, jnp.float32)
        acc[...] = jnp.zeros(acc.shape, jnp.float32)
    weight[...] = jnp.zeros(weight.shape, weight.dtype)
    for copy in copies:
        copy.wait()

    def entries(j):
        return [lists[(which * ITEMS + j) * UNIT + u] for u in range(UNIT)]

    def places(j):
        return [jnp.maximum(e, 0) for e in entries(j)]

    def tile_of(j):
        return tiles[which * ITEMS + j] & (TPD - 1)

    def scores(j):
        d, spots = tile_of(j), places(j)
        for g in range(2):
            k = jnp.concatenate([kv[w, 0:SEG, g * HEAD : (g + 1) * HEAD] for w in spots], axis=0)
            s = jnp.dot(k, qt[d, g], preferred_element_type=jnp.float32)
            score[g] = s
            for u in range(UNIT):
                part = s[u * SEG : (u + 1) * SEG].reshape(SEG // 8, 8, ROWS)
                peak[g, u] = jnp.max(part, axis=0)

        @pl.when(tiles[which * ITEMS + j] >= TPD)
        def _():
            key = lax.broadcasted_iota(jnp.int32, (SEG, ROWS), 0)
            token = lax.broadcasted_iota(jnp.int32, (SEG, ROWS), 1) & (TILE - 1)
            ok = key <= token + (info[d] & 3) * TILE
            for g in range(2):
                s = jnp.where(ok, score[g, 0:SEG], FILL)
                score[g, 0:SEG] = s
                peak[g, 0] = jnp.max(s.reshape(SEG // 8, 8, ROWS), axis=0)

    def add(j, drops):
        d, spots = tile_of(j), places(j)
        for g in range(2):
            v = jnp.concatenate(
                [kv[w, SEG : 2 * SEG, g * HEAD : (g + 1) * HEAD] for w in spots], axis=1
            )
            acc[d * 2 + g] = acc[d * 2 + g] * drops[g] + jnp.dot(
                v, weight[g], preferred_element_type=jnp.float32
            )

    def body(j, drops):
        add(jnp.maximum(j - 1, 0), drops)
        d = tile_of(j)
        pens = [jnp.where(e < 0, 3e31, 0.0) for e in entries(j)]
        result = []
        for g in range(2):
            i = d * 2 + g
            old = top[i]
            peaks = functools.reduce(jnp.maximum, [peak[g, u] - pens[u] for u in range(UNIT)])
            new = jnp.maximum(old, jnp.max(peaks, axis=0, keepdims=True))
            drop = jnp.exp2((old - new) * SCALE)
            part = jnp.zeros((8, ROWS), jnp.float32)
            for u in range(UNIT):
                e = jnp.exp2((score[g, u * SEG : (u + 1) * SEG] - (new + pens[u])) * SCALE)
                part += jnp.sum(e.reshape(SEG // 8, 8, ROWS), axis=0)
                weight[g, u * SEG : (u + 1) * SEG] = e.astype(jnp.bfloat16)
            total[i] = total[i] * drop + jnp.sum(part, axis=0, keepdims=True)
            top[i] = new
            result.append(drop)
        scores(j + 1)
        return tuple(result)

    rounds = counts[which] // UNIT
    ones = jnp.ones((1, ROWS), jnp.float32)
    scores(0)
    drops = lax.fori_loop(0, rounds, body, (ones, ones))
    add(jnp.maximum(rounds - 1, 0), drops)

    if finish:

        def write(d, carry):
            for g in range(2):
                i = d * 2 + g
                o = (acc[i] / total[i]).T.astype(out.dtype)
                for h in range(GROUP):
                    out[
                        pl.ds(pl.multiple_of(d * TILE, TILE), TILE),
                        (g * GROUP + h) * HEAD : (g * GROUP + h + 1) * HEAD,
                    ] = o[h * TILE : (h + 1) * TILE]
            return carry

        lax.fori_loop(0, TPD, write, 0)


def attend(which, work, qt, pieces, state):
    first, finish = which == 0, which == PASSES - 1
    shapes = [
        jax.ShapeDtypeStruct((2 * TPD, 1, ROWS), jnp.float32),
        jax.ShapeDtypeStruct((2 * TPD, 1, ROWS), jnp.float32),
        jax.ShapeDtypeStruct((2 * TPD, HEAD, ROWS), jnp.float32),
    ]
    if finish:
        shapes.append(jax.ShapeDtypeStruct((TPD * TILE, 2 * GROUP * HEAD), jnp.bfloat16))
    blocks = sum(piece.shape[0] for piece in pieces)
    begin = len(work) + 1 + len(pieces)
    return pl.pallas_call(
        functools.partial(attend_kernel, which, len(pieces)),
        in_specs=[smem()] * len(work)
        + [vmem()]
        + [pl.BlockSpec(memory_space=pl.ANY)] * len(pieces)
        + [vmem()] * (0 if first else 3),
        out_specs=[vmem()] * len(shapes),
        out_shape=shapes,
        input_output_aliases={} if first else {begin + n: n for n in range(3)},
        scratch_shapes=[
            pltpu.VMEM((blocks, 2 * SEG, 2 * HEAD), jnp.bfloat16),
            pltpu.VMEM((2, UNIT * SEG, ROWS), jnp.float32),
            pltpu.VMEM((2, UNIT, 8, ROWS), jnp.float32),
            pltpu.VMEM((2, UNIT * SEG, ROWS), jnp.bfloat16),
            pltpu.SemaphoreType.DMA((len(pieces),)),
        ],
        compiler_params=pltpu.CompilerParams(vmem_limit_bytes=28 * MIB),
        cost_estimate=pl.CostEstimate(
            flops=256 * 16 * 128 * 128 * 32, bytes_accessed=6 * MIB, transcendentals=0
        ),
        name="attend",
    )(*work, qt, *pieces, *(() if first else state))


def cat(*parts):
    return jnp.concatenate(parts, axis=0)


def ring_four(block, axis, up, down, also=()):
    half = block.shape[0] // 2
    low = lax.ppermute(block, axis, up)
    high = lax.ppermute(block, axis, down)
    low, high, also = lax.optimization_barrier((low, high, also))
    far0 = lax.ppermute(low[:half], axis, up)
    far1 = lax.ppermute(high[half:], axis, down)
    return [block, low, high, far0, far1], also


def ring_z(block):
    half = block.shape[0] // 2
    parts = [block]
    low = high = block
    for _ in range(3):
        low = lax.ppermute(low, "ctx", ZP)
        high = lax.ppermute(high, "ctx", ZM)
        parts += [low, high]
    return parts + [lax.ppermute(low[:half], "ctx", ZP), lax.ppermute(high[half:], "ctx", ZM)]


def swap(a):
    return lax.ppermute(a, "leaf", CS)


def swapped(*pieces):
    return in_blocks(list(pieces) + [swap(a) for a in pieces])


def in_blocks(pieces):
    return [a.reshape(-1, 2 * SEG, 2 * HEAD) for a in pieces]


def on_device(queries, inputs, key_weight, value_weight, parents, tile_dest):
    leaf, ctx, y = lax.axis_index("leaf"), lax.axis_index("ctx"), lax.axis_index("head")
    where = jnp.stack([leaf, ctx, y]).astype(jnp.int32)
    sends, table, info = pack(where, tile_dest, queries)
    came = {0: sends[0]}
    for s in (2, 6, 3, 5, 1, 7, 4):
        came[s] = lax.ppermute(sends[s], "ctx", turn(NZ, s))
    rows, (came[2], came[6]) = ring_four(inputs, "head", YP, YM, (came[2], came[6]))

    seg = jnp.arange(parents.shape[0], dtype=jnp.int32)
    odd = (seg & 1) == 1
    block = seg >> 1
    from_leaf, from_z = block >> 3, block & (NZ - 1)
    z = (from_z - ctx) & (NZ - 1)
    x = ((from_leaf >> 1) - (leaf >> 1)) & (NX - 1)
    at_z = jnp.where(z == 0, 0, jnp.where(z < 4, 2 * z, jnp.where(z == 4, 7, 2 * (NZ - z) - 1)))
    at_x = jnp.where(x == 0, 0, jnp.where(x == 1, 2, jnp.where(x == 2, 3, 1)))
    which = jnp.where(
        odd,
        jnp.where(z <= 4, z, NZ - z),
        jnp.where(x == 0, 0, jnp.where(x == 3, 2, jnp.where(x == 1, 3, 4))),
    )
    ahead = jnp.where(odd & (z > 0) & (z < 4), 4, 0)
    start_odd = jnp.where(which == 0, 8, ahead)
    start_even = jnp.where(which == 0, 0, jnp.where(which == 4, 4, 8))
    place = jnp.where(odd, start_odd + at_x, start_even + at_z)
    span = jnp.where((which == 0) | (which == 4), 12, jnp.where(which == 1, 8, 16))
    place = place + span * ((from_leaf ^ leaf) & 1)
    work = list(walk(parents, info, which, place))
    rows, work, came[3], came[5] = lax.optimization_barrier((rows, work, came[3], came[5]))
    work.append(info)

    kv = project(where, *rows, key_weight, value_weight)
    half = kv.shape[0] // 2
    odds = cat(*ring_four(kv[half:], "leaf", XP, XM)[0])
    evens, odds, came[1], came[7] = lax.optimization_barrier(
        (kv[:half], odds, came[1], came[7])
    )
    evens = cat(*ring_z(evens))
    qt = unpack(table, [came[s] for s in range(NZ)])

    def along_z(a, b):
        return lax.ppermute(a, "ctx", ZP), lax.ppermute(b, "ctx", ZM)

    low1, high1 = along_z(odds, odds)
    odds_too = swap(odds)
    evens, odds, odds_too, low1, high1, qt = lax.optimization_barrier(
        (evens, odds, odds_too, low1, high1, qt)
    )

    low_x, high_x = lax.ppermute(evens, "leaf", XP), lax.ppermute(evens, "leaf", XM)
    low2, high2 = along_z(low1, high1)
    state = attend(0, work, qt, in_blocks([evens, odds, swap(evens), odds_too]), None)
    low1, high1, low2, high2, state = lax.optimization_barrier((low1, high1, low2, high2, state))
    pieces = swapped(low1, high1)
    low3, high3 = along_z(low2, high2)
    state = attend(1, work, qt, pieces, state)
    low3, high3, low_x, high_x, state = lax.optimization_barrier(
        (low3, high3, low_x, high_x, state)
    )
    pieces = swapped(low2, high2, low_x)
    mid = low_x.shape[0] // 2
    far0 = lax.ppermute(low_x[:mid], "leaf", XP)
    far1 = lax.ppermute(high_x[mid:], "leaf", XM)
    mid = low3.shape[0] // 2
    low4, high4 = along_z(low3[:mid], high3[mid:])
    state = attend(2, work, qt, pieces, state)
    low3, high3, high_x, low4, high4, far0, far1, state = lax.optimization_barrier(
        (low3, high3, high_x, low4, high4, far0, far1, state)
    )
    pieces = swapped(low3, high3, high_x)
    last = swapped(low4, high4, far0, far1)
    state = attend(3, work, qt, pieces, state)
    return attend(4, work, qt, last, state)[3]


def solution(mesh):
    in_specs = (
        P(("leaf", "ctx"), "head"),
        P(("leaf", "ctx"), "head"),
        P(None, "head"),
        P(None, "head"),
        P(),
        P(),
    )
    out_specs = P(("leaf", "ctx"), "head")
    return jax.shard_map(
        on_device, mesh=mesh, in_specs=in_specs, out_specs=out_specs, check_vma=False
    )
```

```python
import functools
import math

import jax
import jax.numpy as jnp
from jax import lax
from jax.experimental import pallas as pl
from jax.experimental.pallas import tpu as pltpu
from jax.sharding import PartitionSpec as P

HEAD = 128
GROUP = 8
SEG = 128
TILE = 32
TPD = 8
CAP = 2
NX, NZ, NY = 4, 8, 4
ROWS = TILE * GROUP
SCALE = math.log2(math.e) / math.sqrt(HEAD)
FILL = -1.2e31
MIB = 1 << 20
UNIT = 4
PASSES = 5
ITEMS = 8 * 32 // UNIT + 4

XP = [(2 * x + c, 2 * ((x + 1) % NX) + c) for x in range(NX) for c in range(2)]
XM = [(2 * x + c, 2 * ((x - 1) % NX) + c) for x in range(NX) for c in range(2)]
CS = [(i, i ^ 1) for i in range(2 * NX)]


def turn(n, by):
    return [(i, (i + by) % n) for i in range(n)]


ZP, ZM = turn(NZ, 1), turn(NZ, -1)
YP, YM = turn(NY, 1), turn(NY, -1)

smem = functools.partial(pl.BlockSpec, memory_space=pltpu.SMEM)
vmem = functools.partial(pl.BlockSpec, memory_space=pltpu.VMEM)


def pack_kernel(where, dest, q, *outs):
    sends, table, info = outs[:NZ], outs[NZ], outs[NZ + 1]
    leaf, ctx = where[0], where[1]
    device = leaf * NZ + ctx
    shifts = [((dest[device * TPD + j] >> 3) - ctx) & (NZ - 1) for j in range(TPD)]
    ranks = []
    for j in range(TPD):
        rank = jnp.int32(0)
        for i in range(j):
            rank = rank + (shifts[i] == shifts[j]).astype(jnp.int32)
        ranks.append(rank)
    for s in range(NZ):
        for r in range(CAP):
            pick = jnp.int32(0)
            for j in range(TPD):
                pick = jnp.where((shifts[j] == s) & (ranks[j] == r), j, pick)
            sends[s][r] = q[pl.ds(pl.multiple_of(pick * TILE, TILE), TILE), :]
    for s in range(NZ):
        base = (leaf * NZ + ((ctx - s) & (NZ - 1))) * TPD
        table[s * CAP] = jnp.int32(-1)
        table[s * CAP + 1] = jnp.int32(-1)

        def one(j, rank, s=s, base=base):
            to = dest[base + j]
            mine = (to >> 3) == device

            @pl.when(mine)
            def _():
                table[s * CAP + rank] = to & (TPD - 1)
                info[to & (TPD - 1)] = base + j

            return rank + mine.astype(jnp.int32)

        lax.fori_loop(0, TPD, one, jnp.int32(0))


def pack(where, dest, q):
    width = q.shape[1]
    outs = pl.pallas_call(
        pack_kernel,
        in_specs=[smem(), smem(), vmem()],
        out_specs=[vmem()] * NZ + [smem(), smem()],
        out_shape=[jax.ShapeDtypeStruct((CAP, TILE, width), q.dtype)] * NZ
        + [jax.ShapeDtypeStruct((NZ * CAP,), jnp.int32), jax.ShapeDtypeStruct((TPD,), jnp.int32)],
        compiler_params=pltpu.CompilerParams(vmem_limit_bytes=32 * MIB),
        cost_estimate=pl.CostEstimate(flops=0, bytes_accessed=3 * MIB, transcendentals=0),
        name="pack",
    )(where, dest, q)
    return outs[:NZ], outs[NZ], outs[NZ + 1]


def walk_kernel(parents, info, which, place, lists, tiles, counts):
    for p in range(PASSES):
        counts[p] = jnp.int32(0)

    def tile(d, carry):
        seg = info[d] >> 2

        def body(at):
            p = which[at]
            used = counts[p]

            @pl.when((used & (UNIT - 1)) == 0)
            def _():
                tiles[p * ITEMS + used // UNIT] = d + jnp.where(at == seg, TPD, 0)

            lists[p * ITEMS * UNIT + used] = place[at]
            counts[p] = used + 1
            return parents[at]

        lax.while_loop(lambda at: at >= 0, body, seg)
        for p in range(PASSES):
            used = counts[p]
            for n in range(UNIT):
                lists[p * ITEMS * UNIT + used + n] = jnp.int32(-1)
            counts[p] = ((used + UNIT - 1) // UNIT) * UNIT
        return carry

    lax.fori_loop(0, TPD, tile, 0)
    for p in range(PASSES):
        used = counts[p]
        tiles[p * ITEMS + used // UNIT] = jnp.int32(0)
        for n in range(UNIT):
            lists[p * ITEMS * UNIT + used + n] = jnp.int32(-1)


def walk(parents, info, which, place):
    return pl.pallas_call(
        walk_kernel,
        in_specs=[smem()] * 4,
        out_specs=[smem()] * 3,
        out_shape=[
            jax.ShapeDtypeStruct((PASSES * ITEMS * UNIT,), jnp.int32),
            jax.ShapeDtypeStruct((PASSES * ITEMS,), jnp.int32),
            jax.ShapeDtypeStruct((PASSES,), jnp.int32),
        ],
        cost_estimate=pl.CostEstimate(flops=0, bytes_accessed=16 * MIB, transcendentals=0),
        name="walk",
    )(parents, info, which, place)


def unpack_kernel(table, *refs):
    came, out = refs[:NZ], refs[NZ]
    for s in range(NZ):

        def one(r, carry, s=s):
            d = table[s * CAP + r]

            @pl.when(d >= 0)
            def _():
                for g in range(2):
                    heads = [
                        came[s][r, :, pl.ds((g * GROUP + h) * HEAD, HEAD)] for h in range(GROUP)
                    ]
                    out[d, g] = jnp.concatenate(heads, axis=0).T

            return carry

        lax.fori_loop(0, CAP, one, 0)


def unpack(table, came):
    return pl.pallas_call(
        unpack_kernel,
        in_specs=[smem()] + [vmem()] * NZ,
        out_specs=vmem(),
        out_shape=jax.ShapeDtypeStruct((TPD, 2, HEAD, ROWS), jnp.bfloat16),
        compiler_params=pltpu.CompilerParams(vmem_limit_bytes=32 * MIB),
        cost_estimate=pl.CostEstimate(flops=0, bytes_accessed=6 * MIB, transcendentals=0),
        name="unpack",
    )(table, *came)


def project_kernel(where, own, before, after, far0, far1, wk, wv, out):
    y = where[2]
    depth = own.shape[1]
    half = far0.shape[0]

    def rows(by):
        at = (y + by) & (NY - 1)
        return pl.ds(pl.multiple_of(at * depth, depth), depth)

    def times(w):
        total = jnp.dot(own[...], w[rows(0), :], preferred_element_type=jnp.float32)
        total += jnp.dot(before[...], w[rows(NY - 1), :], preferred_element_type=jnp.float32)
        total += jnp.dot(after[...], w[rows(1), :], preferred_element_type=jnp.float32)
        far = jnp.concatenate([far0[...], far1[...]], axis=0)
        return total + jnp.dot(far, w[rows(2), :], preferred_element_type=jnp.float32)

    k = times(wk)
    v = times(wv)
    for n in range(2):
        at = n * 2 * SEG
        out[at : at + SEG, :] = k[n * SEG : (n + 1) * SEG].astype(out.dtype)
        for g in range(2):
            part = v[n * SEG : (n + 1) * SEG, g * HEAD : (g + 1) * HEAD]
            out[at + SEG : at + 2 * SEG, g * HEAD : (g + 1) * HEAD] = part.T.astype(out.dtype)


def project(where, own, before, after, far0, far1, wk, wv):
    return pl.pallas_call(
        project_kernel,
        in_specs=[smem()] + [vmem()] * 7,
        out_specs=vmem(),
        out_shape=jax.ShapeDtypeStruct((4 * SEG, 2 * HEAD), jnp.bfloat16),
        compiler_params=pltpu.CompilerParams(vmem_limit_bytes=40 * MIB),
        cost_estimate=pl.CostEstimate(flops=2 * 256 * 5120 * 512, bytes_accessed=8 * MIB, transcendentals=0),
        name="project",
    )(where, own, before, after, far0, far1, wk, wv)


def attend_kernel(which, n_pieces, lists, tiles, counts, info, qt, *refs):
    pieces, refs = refs[:n_pieces], refs[n_pieces:]
    first, finish = which == 0, which == PASSES - 1
    if not first:
        refs = refs[3:]
    top, total, acc = refs[:3]
    if finish:
        out, kv, score, peak, weight, sems = refs[3:]
    else:
        kv, score, peak, weight, sems = refs[3:]
    copies, at = [], 0
    for n, piece in enumerate(pieces):
        size = piece.shape[0]
        copies.append(pltpu.make_async_copy(piece, kv.at[pl.ds(at, size)], sems.at[n]))
        at += size
    for copy in copies:
        copy.start()
    if first:
        top[...] = jnp.full(top.shape, FILL, jnp.float32)
        total[...] = jnp.zeros(total.shape, jnp.float32)
        acc[...] = jnp.zeros(acc.shape, jnp.float32)
    weight[...] = jnp.zeros(weight.shape, weight.dtype)
    for copy in copies:
        copy.wait()

    def entries(j):
        return [lists[(which * ITEMS + j) * UNIT + u] for u in range(UNIT)]

    def places(j):
        return [jnp.maximum(e, 0) for e in entries(j)]

    def tile_of(j):
        return tiles[which * ITEMS + j] & (TPD - 1)

    def scores(j):
        d, spots = tile_of(j), places(j)
        for g in range(2):
            k = jnp.concatenate([kv[w, 0:SEG, g * HEAD : (g + 1) * HEAD] for w in spots], axis=0)
            s = jnp.dot(k, qt[d, g], preferred_element_type=jnp.float32)
            score[g] = s
            for u in range(UNIT):
                part = s[u * SEG : (u + 1) * SEG].reshape(SEG // 8, 8, ROWS)
                peak[g, u] = jnp.max(part, axis=0)

        @pl.when(tiles[which * ITEMS + j] >= TPD)
        def _():
            key = lax.broadcasted_iota(jnp.int32, (SEG, ROWS), 0)
            token = lax.broadcasted_iota(jnp.int32, (SEG, ROWS), 1) & (TILE - 1)
            ok = key <= token + (info[d] & 3) * TILE
            for g in range(2):
                s = jnp.where(ok, score[g, 0:SEG], FILL)
                score[g, 0:SEG] = s
                peak[g, 0] = jnp.max(s.reshape(SEG // 8, 8, ROWS), axis=0)

    def add(j, drops):
        d, spots = tile_of(j), places(j)
        for g in range(2):
            v = jnp.concatenate(
                [kv[w, SEG : 2 * SEG, g * HEAD : (g + 1) * HEAD] for w in spots], axis=1
            )
            acc[d * 2 + g] = acc[d * 2 + g] * drops[g] + jnp.dot(
                v, weight[g], preferred_element_type=jnp.float32
            )

    def body(j, drops):
        add(jnp.maximum(j - 1, 0), drops)
        d = tile_of(j)
        pens = [jnp.where(e < 0, 3e31, 0.0) for e in entries(j)]
        result = []
        for g in range(2):
            i = d * 2 + g
            old = top[i]
            peaks = functools.reduce(jnp.maximum, [peak[g, u] - pens[u] for u in range(UNIT)])
            new = jnp.maximum(old, jnp.max(peaks, axis=0, keepdims=True))
            drop = jnp.exp2((old - new) * SCALE)
            part = jnp.zeros((8, ROWS), jnp.float32)
            for u in range(UNIT):
                e = jnp.exp2((score[g, u * SEG : (u + 1) * SEG] - (new + pens[u])) * SCALE)
                part += jnp.sum(e.reshape(SEG // 8, 8, ROWS), axis=0)
                weight[g, u * SEG : (u + 1) * SEG] = e.astype(jnp.bfloat16)
            total[i] = total[i] * drop + jnp.sum(part, axis=0, keepdims=True)
            top[i] = new
            result.append(drop)
        scores(j + 1)
        return tuple(result)

    rounds = counts[which] // UNIT
    ones = jnp.ones((1, ROWS), jnp.float32)
    scores(0)
    drops = lax.fori_loop(0, rounds, body, (ones, ones))
    add(jnp.maximum(rounds - 1, 0), drops)

    if finish:

        def write(d, carry):
            for g in range(2):
                i = d * 2 + g
                o = (acc[i] / total[i]).T.astype(out.dtype)
                for h in range(GROUP):
                    out[
                        pl.ds(pl.multiple_of(d * TILE, TILE), TILE),
                        (g * GROUP + h) * HEAD : (g * GROUP + h + 1) * HEAD,
                    ] = o[h * TILE : (h + 1) * TILE]
            return carry

        lax.fori_loop(0, TPD, write, 0)


def attend(which, work, qt, pieces, state):
    first, finish = which == 0, which == PASSES - 1
    shapes = [
        jax.ShapeDtypeStruct((2 * TPD, 1, ROWS), jnp.float32),
        jax.ShapeDtypeStruct((2 * TPD, 1, ROWS), jnp.float32),
        jax.ShapeDtypeStruct((2 * TPD, HEAD, ROWS), jnp.float32),
    ]
    if finish:
        shapes.append(jax.ShapeDtypeStruct((TPD * TILE, 2 * GROUP * HEAD), jnp.bfloat16))
    blocks = sum(piece.shape[0] for piece in pieces)
    begin = len(work) + 1 + len(pieces)
    return pl.pallas_call(
        functools.partial(attend_kernel, which, len(pieces)),
        in_specs=[smem()] * len(work)
        + [vmem()]
        + [pl.BlockSpec(memory_space=pl.ANY)] * len(pieces)
        + [vmem()] * (0 if first else 3),
        out_specs=[vmem()] * len(shapes),
        out_shape=shapes,
        input_output_aliases={} if first else {begin + n: n for n in range(3)},
        scratch_shapes=[
            pltpu.VMEM((blocks, 2 * SEG, 2 * HEAD), jnp.bfloat16),
            pltpu.VMEM((2, UNIT * SEG, ROWS), jnp.float32),
            pltpu.VMEM((2, UNIT, 8, ROWS), jnp.float32),
            pltpu.VMEM((2, UNIT * SEG, ROWS), jnp.bfloat16),
            pltpu.SemaphoreType.DMA((len(pieces),)),
        ],
        compiler_params=pltpu.CompilerParams(vmem_limit_bytes=28 * MIB),
        cost_estimate=pl.CostEstimate(
            flops=256 * 16 * 128 * 128 * 32, bytes_accessed=6 * MIB, transcendentals=0
        ),
        name="attend",
    )(*work, qt, *pieces, *(() if first else state))


def cat(*parts):
    return jnp.concatenate(parts, axis=0)


def ring_four(block, axis, up, down, also=()):
    half = block.shape[0] // 2
    low = lax.ppermute(block, axis, up)
    high = lax.ppermute(block, axis, down)
    low, high, also = lax.optimization_barrier((low, high, also))
    far0 = lax.ppermute(low[:half], axis, up)
    far1 = lax.ppermute(high[half:], axis, down)
    return [block, low, high, far0, far1], also


def along_z(a, b):
    return lax.ppermute(a, "ctx", ZP), lax.ppermute(b, "ctx", ZM)


def swap(a):
    return lax.ppermute(a, "leaf", CS)


def swapped(*pieces):
    return in_blocks(list(pieces) + [swap(a) for a in pieces])


def in_blocks(pieces):
    return [a.reshape(-1, 2 * SEG, 2 * HEAD) for a in pieces]


def on_device(queries, inputs, key_weight, value_weight, parents, tile_dest):
    leaf, ctx, y = lax.axis_index("leaf"), lax.axis_index("ctx"), lax.axis_index("head")
    where = jnp.stack([leaf, ctx, y]).astype(jnp.int32)
    sends, table, info = pack(where, tile_dest, queries)
    came = {0: sends[0]}
    for s in (1, 7, 3, 5, 2, 6, 4):
        came[s] = lax.ppermute(sends[s], "ctx", turn(NZ, s))
    rows, (came[1], came[7]) = ring_four(inputs, "head", YP, YM, (came[1], came[7]))

    seg = jnp.arange(parents.shape[0], dtype=jnp.int32)
    odd = (seg & 1) == 1
    block = seg >> 1
    from_leaf, from_z = block >> 3, block & (NZ - 1)
    z = (from_z - ctx) & (NZ - 1)
    x = ((from_leaf >> 1) - (leaf >> 1)) & (NX - 1)
    at_z = jnp.where(z == 0, 0, jnp.where(z < 4, 2 * z, jnp.where(z == 4, 7, 2 * (NZ - z) - 1)))
    at_x = jnp.where(x == 0, 0, jnp.where(x == 1, 2, jnp.where(x == 2, 3, 1)))
    which = jnp.where(
        odd,
        jnp.where(z <= 4, z, NZ - z),
        jnp.where(x == 0, 1, jnp.where(x == 3, 2, jnp.where(x == 1, 3, 4))),
    )
    ahead = jnp.where(odd & (z > 0) & (z < 4), 4, 0)
    start_odd = jnp.where(which == 1, 8, 0) + ahead
    start_even = jnp.where(which == 1, 0, jnp.where(which == 4, 4, 8))
    place = jnp.where(odd, start_odd + at_x, start_even + at_z)
    span = jnp.where(which == 0, 4, jnp.where(which == 4, 12, 16))
    place = place + span * ((from_leaf ^ leaf) & 1)
    work = list(walk(parents, info, which, place))
    rows, work, came[3], came[5] = lax.optimization_barrier((rows, work, came[3], came[5]))
    work.append(info)

    kv = project(where, *rows, key_weight, value_weight)
    half = kv.shape[0] // 2
    odds = cat(*ring_four(kv[half:], "leaf", XP, XM)[0])
    block, odds, came[2], came[6] = lax.optimization_barrier((kv[:half], odds, came[2], came[6]))
    qt = unpack(table, [came[s] for s in range(NZ)])
    state = attend(0, work, qt, in_blocks([odds, swap(odds)]), None)

    parts, low, high = [block], block, block
    for _ in range(3):
        low, high = along_z(low, high)
        parts += [low, high]
    low, high, state = lax.optimization_barrier((low, high, state))
    mid = low.shape[0] // 2
    evens = cat(*parts, *along_z(low[:mid], high[mid:]))
    low1, high1 = along_z(odds, odds)
    too1 = [swap(low1), swap(high1)]
    evens, low1, high1, too1, state = lax.optimization_barrier((evens, low1, high1, too1, state))

    low_x, high_x = lax.ppermute(evens, "leaf", XP), lax.ppermute(evens, "leaf", XM)
    low2, high2 = along_z(low1, high1)
    pieces = in_blocks([evens, low1, high1, swap(evens)] + too1)
    state = attend(1, work, qt, pieces, state)
    low2, high2, low_x, high_x, state = lax.optimization_barrier(
        (low2, high2, low_x, high_x, state)
    )
    pieces = swapped(low2, high2, low_x)
    mid = low_x.shape[0] // 2
    far0 = lax.ppermute(low_x[:mid], "leaf", XP)
    far1 = lax.ppermute(high_x[mid:], "leaf", XM)
    low3, high3 = along_z(low2, high2)
    state = attend(2, work, qt, pieces, state)
    low3, high3, high_x, far0, far1, state = lax.optimization_barrier(
        (low3, high3, high_x, far0, far1, state)
    )
    mid = low3.shape[0] // 2
    low4, high4 = along_z(low3[:mid], high3[mid:])
    state = attend(3, work, qt, swapped(low3, high3, high_x), state)
    low4, high4, far0, far1, state = lax.optimization_barrier((low4, high4, far0, far1, state))
    return attend(4, work, qt, swapped(low4, high4, far0, far1), state)[3]


def solution(mesh):
    in_specs = (
        P(("leaf", "ctx"), "head"),
        P(("leaf", "ctx"), "head"),
        P(None, "head"),
        P(None, "head"),
        P(),
        P(),
    )
    out_specs = P(("leaf", "ctx"), "head")
    return jax.shard_map(
        on_device, mesh=mesh, in_specs=in_specs, out_specs=out_specs, check_vma=False
    )
```

```python
import functools
import math

import jax
import jax.numpy as jnp
from jax import lax
from jax.experimental import pallas as pl
from jax.experimental.pallas import tpu as pltpu
from jax.sharding import PartitionSpec as P

HEAD = 128
GROUP = 8
SEG = 128
TILE = 32
TPD = 8
CAP = 2
NX, NZ, NY = 4, 8, 4
ROWS = TILE * GROUP
SCALE = math.log2(math.e) / math.sqrt(HEAD)
FILL = -1.2e31
MIB = 1 << 20
UNIT = 4
PASSES = 5
ITEMS = 8 * 32 // UNIT + 4

XP = [(2 * x + c, 2 * ((x + 1) % NX) + c) for x in range(NX) for c in range(2)]
XM = [(2 * x + c, 2 * ((x - 1) % NX) + c) for x in range(NX) for c in range(2)]
CS = [(i, i ^ 1) for i in range(2 * NX)]


def turn(n, by):
    return [(i, (i + by) % n) for i in range(n)]


ZP, ZM = turn(NZ, 1), turn(NZ, -1)
YP, YM = turn(NY, 1), turn(NY, -1)

smem = functools.partial(pl.BlockSpec, memory_space=pltpu.SMEM)
vmem = functools.partial(pl.BlockSpec, memory_space=pltpu.VMEM)


def pack_kernel(where, dest, q, *outs):
    sends, table, info = outs[:NZ], outs[NZ], outs[NZ + 1]
    leaf, ctx = where[0], where[1]
    device = leaf * NZ + ctx
    shifts = [((dest[device * TPD + j] >> 3) - ctx) & (NZ - 1) for j in range(TPD)]
    ranks = []
    for j in range(TPD):
        rank = jnp.int32(0)
        for i in range(j):
            rank = rank + (shifts[i] == shifts[j]).astype(jnp.int32)
        ranks.append(rank)
    for s in range(NZ):
        for r in range(CAP):
            pick = jnp.int32(0)
            for j in range(TPD):
                pick = jnp.where((shifts[j] == s) & (ranks[j] == r), j, pick)
            sends[s][r] = q[pl.ds(pl.multiple_of(pick * TILE, TILE), TILE), :]
    for s in range(NZ):
        base = (leaf * NZ + ((ctx - s) & (NZ - 1))) * TPD
        table[s * CAP] = jnp.int32(-1)
        table[s * CAP + 1] = jnp.int32(-1)

        def one(j, rank, s=s, base=base):
            to = dest[base + j]
            mine = (to >> 3) == device

            @pl.when(mine)
            def _():
                table[s * CAP + rank] = to & (TPD - 1)
                info[to & (TPD - 1)] = base + j

            return rank + mine.astype(jnp.int32)

        lax.fori_loop(0, TPD, one, jnp.int32(0))


def pack(where, dest, q):
    width = q.shape[1]
    outs = pl.pallas_call(
        pack_kernel,
        in_specs=[smem(), smem(), vmem()],
        out_specs=[vmem()] * NZ + [smem(), smem()],
        out_shape=[jax.ShapeDtypeStruct((CAP, TILE, width), q.dtype)] * NZ
        + [jax.ShapeDtypeStruct((NZ * CAP,), jnp.int32), jax.ShapeDtypeStruct((TPD,), jnp.int32)],
        compiler_params=pltpu.CompilerParams(vmem_limit_bytes=32 * MIB),
        cost_estimate=pl.CostEstimate(flops=0, bytes_accessed=3 * MIB, transcendentals=0),
        name="pack",
    )(where, dest, q)
    return outs[:NZ], outs[NZ], outs[NZ + 1]


def walk_kernel(parents, info, which, place, lists, tiles, counts):
    for p in range(PASSES):
        counts[p] = jnp.int32(0)

    def tile(d, carry):
        seg = info[d] >> 2

        def body(at):
            p = which[at]
            used = counts[p]

            @pl.when((used & (UNIT - 1)) == 0)
            def _():
                tiles[p * ITEMS + used // UNIT] = d + jnp.where(at == seg, TPD, 0)

            lists[p * ITEMS * UNIT + used] = place[at]
            counts[p] = used + 1
            return parents[at]

        lax.while_loop(lambda at: at >= 0, body, seg)
        for p in range(PASSES):
            used = counts[p]
            for n in range(UNIT):
                lists[p * ITEMS * UNIT + used + n] = jnp.int32(-1)
            counts[p] = ((used + UNIT - 1) // UNIT) * UNIT
        return carry

    lax.fori_loop(0, TPD, tile, 0)
    for p in range(PASSES):
        used = counts[p]
        tiles[p * ITEMS + used // UNIT] = jnp.int32(0)
        for n in range(UNIT):
            lists[p * ITEMS * UNIT + used + n] = jnp.int32(-1)


def walk(parents, info, which, place):
    return pl.pallas_call(
        walk_kernel,
        in_specs=[smem()] * 4,
        out_specs=[smem()] * 3,
        out_shape=[
            jax.ShapeDtypeStruct((PASSES * ITEMS * UNIT,), jnp.int32),
            jax.ShapeDtypeStruct((PASSES * ITEMS,), jnp.int32),
            jax.ShapeDtypeStruct((PASSES,), jnp.int32),
        ],
        cost_estimate=pl.CostEstimate(flops=0, bytes_accessed=16 * MIB, transcendentals=0),
        name="walk",
    )(parents, info, which, place)


def unpack_kernel(table, *refs):
    came, out = refs[:NZ], refs[NZ]
    for s in range(NZ):

        def one(r, carry, s=s):
            d = table[s * CAP + r]

            @pl.when(d >= 0)
            def _():
                for g in range(2):
                    heads = [
                        came[s][r, :, pl.ds((g * GROUP + h) * HEAD, HEAD)] for h in range(GROUP)
                    ]
                    out[d, g] = jnp.concatenate(heads, axis=0).T

            return carry

        lax.fori_loop(0, CAP, one, 0)


def unpack(table, came):
    return pl.pallas_call(
        unpack_kernel,
        in_specs=[smem()] + [vmem()] * NZ,
        out_specs=vmem(),
        out_shape=jax.ShapeDtypeStruct((TPD, 2, HEAD, ROWS), jnp.bfloat16),
        compiler_params=pltpu.CompilerParams(vmem_limit_bytes=32 * MIB),
        cost_estimate=pl.CostEstimate(flops=0, bytes_accessed=6 * MIB, transcendentals=0),
        name="unpack",
    )(table, *came)


def project_kernel(where, own, before, after, far0, far1, wk, wv, out):
    y = where[2]
    depth = own.shape[1]
    half = far0.shape[0]

    def rows(by):
        at = (y + by) & (NY - 1)
        return pl.ds(pl.multiple_of(at * depth, depth), depth)

    def times(w):
        total = jnp.dot(own[...], w[rows(0), :], preferred_element_type=jnp.float32)
        total += jnp.dot(before[...], w[rows(NY - 1), :], preferred_element_type=jnp.float32)
        total += jnp.dot(after[...], w[rows(1), :], preferred_element_type=jnp.float32)
        far = jnp.concatenate([far0[...], far1[...]], axis=0)
        return total + jnp.dot(far, w[rows(2), :], preferred_element_type=jnp.float32)

    k = times(wk)
    v = times(wv)
    for n in range(2):
        at = n * 2 * SEG
        out[at : at + SEG, :] = k[n * SEG : (n + 1) * SEG].astype(out.dtype)
        for g in range(2):
            part = v[n * SEG : (n + 1) * SEG, g * HEAD : (g + 1) * HEAD]
            out[at + SEG : at + 2 * SEG, g * HEAD : (g + 1) * HEAD] = part.T.astype(out.dtype)


def project(where, own, before, after, far0, far1, wk, wv):
    return pl.pallas_call(
        project_kernel,
        in_specs=[smem()] + [vmem()] * 7,
        out_specs=vmem(),
        out_shape=jax.ShapeDtypeStruct((4 * SEG, 2 * HEAD), jnp.bfloat16),
        compiler_params=pltpu.CompilerParams(vmem_limit_bytes=40 * MIB),
        cost_estimate=pl.CostEstimate(flops=2 * 256 * 5120 * 512, bytes_accessed=8 * MIB, transcendentals=0),
        name="project",
    )(where, own, before, after, far0, far1, wk, wv)


def attend_kernel(which, n_pieces, lists, tiles, counts, info, qt, *refs):
    pieces, refs = refs[:n_pieces], refs[n_pieces:]
    first, finish = which == 0, which == PASSES - 1
    if not first:
        refs = refs[3:]
    top, total, acc = refs[:3]
    if finish:
        out, kv, score, peak, weight, sems = refs[3:]
    else:
        kv, score, peak, weight, sems = refs[3:]
    copies, at = [], 0
    for n, piece in enumerate(pieces):
        size = piece.shape[0]
        copies.append(pltpu.make_async_copy(piece, kv.at[pl.ds(at, size)], sems.at[n]))
        at += size
    for copy in copies:
        copy.start()
    if first:
        top[...] = jnp.full(top.shape, FILL, jnp.float32)
        total[...] = jnp.zeros(total.shape, jnp.float32)
        acc[...] = jnp.zeros(acc.shape, jnp.float32)
    weight[...] = jnp.zeros(weight.shape, weight.dtype)
    for copy in copies:
        copy.wait()

    def entries(j):
        return [lists[(which * ITEMS + j) * UNIT + u] for u in range(UNIT)]

    def places(j):
        return [jnp.maximum(e, 0) for e in entries(j)]

    def tile_of(j):
        return tiles[which * ITEMS + j] & (TPD - 1)

    def scores(j):
        d, spots = tile_of(j), places(j)
        for g in range(2):
            k = jnp.concatenate([kv[w, 0:SEG, g * HEAD : (g + 1) * HEAD] for w in spots], axis=0)
            s = jnp.dot(k, qt[d, g], preferred_element_type=jnp.float32)
            score[g] = s
            for u in range(UNIT):
                part = s[u * SEG : (u + 1) * SEG].reshape(SEG // 8, 8, ROWS)
                peak[g, u] = jnp.max(part, axis=0)

        @pl.when(tiles[which * ITEMS + j] >= TPD)
        def _():
            key = lax.broadcasted_iota(jnp.int32, (SEG, ROWS), 0)
            token = lax.broadcasted_iota(jnp.int32, (SEG, ROWS), 1) & (TILE - 1)
            ok = key <= token + (info[d] & 3) * TILE
            for g in range(2):
                s = jnp.where(ok, score[g, 0:SEG], FILL)
                score[g, 0:SEG] = s
                peak[g, 0] = jnp.max(s.reshape(SEG // 8, 8, ROWS), axis=0)

    def add(j, drops):
        d, spots = tile_of(j), places(j)
        for g in range(2):
            v = jnp.concatenate(
                [kv[w, SEG : 2 * SEG, g * HEAD : (g + 1) * HEAD] for w in spots], axis=1
            )
            acc[d * 2 + g] = acc[d * 2 + g] * drops[g] + jnp.dot(
                v, weight[g], preferred_element_type=jnp.float32
            )

    def body(j, drops):
        add(jnp.maximum(j - 1, 0), drops)
        d = tile_of(j)
        pens = [jnp.where(e < 0, 3e31, 0.0) for e in entries(j)]
        result = []
        for g in range(2):
            i = d * 2 + g
            old = top[i]
            peaks = functools.reduce(jnp.maximum, [peak[g, u] - pens[u] for u in range(UNIT)])
            new = jnp.maximum(old, jnp.max(peaks, axis=0, keepdims=True))
            drop = jnp.exp2((old - new) * SCALE)
            part = jnp.zeros((8, ROWS), jnp.float32)
            for u in range(UNIT):
                e = jnp.exp2((score[g, u * SEG : (u + 1) * SEG] - (new + pens[u])) * SCALE)
                part += jnp.sum(e.reshape(SEG // 8, 8, ROWS), axis=0)
                weight[g, u * SEG : (u + 1) * SEG] = e.astype(jnp.bfloat16)
            total[i] = total[i] * drop + jnp.sum(part, axis=0, keepdims=True)
            top[i] = new
            result.append(drop)
        scores(j + 1)
        return tuple(result)

    rounds = counts[which] // UNIT
    ones = jnp.ones((1, ROWS), jnp.float32)
    scores(0)
    drops = lax.fori_loop(0, rounds, body, (ones, ones))
    add(jnp.maximum(rounds - 1, 0), drops)

    if finish:

        def write(d, carry):
            for g in range(2):
                i = d * 2 + g
                o = (acc[i] / total[i]).T.astype(out.dtype)
                for h in range(GROUP):
                    out[
                        pl.ds(pl.multiple_of(d * TILE, TILE), TILE),
                        (g * GROUP + h) * HEAD : (g * GROUP + h + 1) * HEAD,
                    ] = o[h * TILE : (h + 1) * TILE]
            return carry

        lax.fori_loop(0, TPD, write, 0)


def attend(which, work, qt, pieces, state):
    first, finish = which == 0, which == PASSES - 1
    shapes = [
        jax.ShapeDtypeStruct((2 * TPD, 1, ROWS), jnp.float32),
        jax.ShapeDtypeStruct((2 * TPD, 1, ROWS), jnp.float32),
        jax.ShapeDtypeStruct((2 * TPD, HEAD, ROWS), jnp.float32),
    ]
    if finish:
        shapes.append(jax.ShapeDtypeStruct((TPD * TILE, 2 * GROUP * HEAD), jnp.bfloat16))
    blocks = sum(piece.shape[0] for piece in pieces)
    begin = len(work) + 1 + len(pieces)
    return pl.pallas_call(
        functools.partial(attend_kernel, which, len(pieces)),
        in_specs=[smem()] * len(work)
        + [vmem()]
        + [pl.BlockSpec(memory_space=pl.ANY)] * len(pieces)
        + [vmem()] * (0 if first else 3),
        out_specs=[vmem()] * len(shapes),
        out_shape=shapes,
        input_output_aliases={} if first else {begin + n: n for n in range(3)},
        scratch_shapes=[
            pltpu.VMEM((blocks, 2 * SEG, 2 * HEAD), jnp.bfloat16),
            pltpu.VMEM((2, UNIT * SEG, ROWS), jnp.float32),
            pltpu.VMEM((2, UNIT, 8, ROWS), jnp.float32),
            pltpu.VMEM((2, UNIT * SEG, ROWS), jnp.bfloat16),
            pltpu.SemaphoreType.DMA((len(pieces),)),
        ],
        compiler_params=pltpu.CompilerParams(vmem_limit_bytes=28 * MIB),
        cost_estimate=pl.CostEstimate(
            flops=256 * 16 * 128 * 128 * 32, bytes_accessed=6 * MIB, transcendentals=0
        ),
        name="attend",
    )(*work, qt, *pieces, *(() if first else state))


def cat(*parts):
    return jnp.concatenate(parts, axis=0)


def ring_four(block, axis, up, down, also=()):
    half = block.shape[0] // 2
    low = lax.ppermute(block, axis, up)
    high = lax.ppermute(block, axis, down)
    low, high, also = lax.optimization_barrier((low, high, also))
    far0 = lax.ppermute(low[:half], axis, up)
    far1 = lax.ppermute(high[half:], axis, down)
    return [block, low, high, far0, far1], also


def along_z(a, b):
    return lax.ppermute(a, "ctx", ZP), lax.ppermute(b, "ctx", ZM)


def swap(a):
    return lax.ppermute(a, "leaf", CS)


def swapped(*pieces):
    return in_blocks(list(pieces) + [swap(a) for a in pieces])


def in_blocks(pieces):
    return [a.reshape(-1, 2 * SEG, 2 * HEAD) for a in pieces]


def on_device(queries, inputs, key_weight, value_weight, parents, tile_dest):
    leaf, ctx, y = lax.axis_index("leaf"), lax.axis_index("ctx"), lax.axis_index("head")
    where = jnp.stack([leaf, ctx, y]).astype(jnp.int32)
    sends, table, info = pack(where, tile_dest, queries)
    came = {0: sends[0]}
    for s in (1, 7, 4, 5, 3, 6, 2):
        came[s] = lax.ppermute(sends[s], "ctx", turn(NZ, s))
    rows, (came[1], came[7]) = ring_four(inputs, "head", YP, YM, (came[1], came[7]))

    seg = jnp.arange(parents.shape[0], dtype=jnp.int32)
    block = seg >> 1
    from_leaf, from_z = block >> 3, block & (NZ - 1)
    z = (from_z - ctx) & (NZ - 1)
    x = ((from_leaf >> 1) - (leaf >> 1)) & (NX - 1)
    at_x = jnp.where(x == 0, 0, jnp.where(x == 1, 2, jnp.where(x == 2, 3, 1)))
    which = jnp.where(z <= 4, z, NZ - z)
    ahead = jnp.where((z > 0) & (z < 4), 8, 0)
    span = jnp.where((which == 0) | (which == 4), 8, 16)
    place = at_x * 2 + (seg & 1) + ahead + span * ((from_leaf ^ leaf) & 1)
    work = list(walk(parents, info, which, place))
    rows, work, came[4], came[5] = lax.optimization_barrier((rows, work, came[4], came[5]))
    work.append(info)

    kv = project(where, *rows, key_weight, value_weight)
    plane = cat(*ring_four(kv, "leaf", XP, XM)[0])
    plane, came[2], came[3], came[6] = lax.optimization_barrier(
        (plane, came[2], came[3], came[6])
    )
    qt = unpack(table, [came[s] for s in range(NZ)])

    low, high = along_z(plane, plane)
    state = attend(0, work, qt, swapped(plane), None)
    for p in range(1, PASSES - 1):
        low, high, state = lax.optimization_barrier((low, high, state))
        pieces = swapped(low, high)
        if p == PASSES - 2:
            half = plane.shape[0] // 2
            low, high = low[:half], high[half:]
        low, high = along_z(low, high)
        state = attend(p, work, qt, pieces, state)
    low, high, state = lax.optimization_barrier((low, high, state))
    return attend(PASSES - 1, work, qt, swapped(low, high), state)[3]


def solution(mesh):
    in_specs = (
        P(("leaf", "ctx"), "head"),
        P(("leaf", "ctx"), "head"),
        P(None, "head"),
        P(None, "head"),
        P(),
        P(),
    )
    out_specs = P(("leaf", "ctx"), "head")
    return jax.shard_map(
        on_device, mesh=mesh, in_specs=in_specs, out_specs=out_specs, check_vma=False
    )
```

```python
import functools
import math

import jax
import jax.numpy as jnp
from jax import lax
from jax.experimental import pallas as pl
from jax.experimental.pallas import tpu as pltpu
from jax.sharding import PartitionSpec as P

HEAD = 128
GROUP = 8
SEG = 128
TILE = 32
TPD = 8
CAP = 2
NX, NZ, NY = 4, 8, 4
ROWS = TILE * GROUP
SCALE = math.log2(math.e) / math.sqrt(HEAD)
FILL = -1.2e31
MIB = 1 << 20
UNIT = 4
PASSES = 5
ITEMS = 8 * 32 // UNIT + 4

XP = [(2 * x + c, 2 * ((x + 1) % NX) + c) for x in range(NX) for c in range(2)]
XM = [(2 * x + c, 2 * ((x - 1) % NX) + c) for x in range(NX) for c in range(2)]
CS = [(i, i ^ 1) for i in range(2 * NX)]


def turn(n, by):
    return [(i, (i + by) % n) for i in range(n)]


ZP, ZM = turn(NZ, 1), turn(NZ, -1)
YP, YM = turn(NY, 1), turn(NY, -1)

smem = functools.partial(pl.BlockSpec, memory_space=pltpu.SMEM)
vmem = functools.partial(pl.BlockSpec, memory_space=pltpu.VMEM)


def pack_kernel(where, dest, q, *outs):
    sends, table, info = outs[:NZ], outs[NZ], outs[NZ + 1]
    leaf, ctx = where[0], where[1]
    device = leaf * NZ + ctx
    shifts = [((dest[device * TPD + j] >> 3) - ctx) & (NZ - 1) for j in range(TPD)]
    ranks = []
    for j in range(TPD):
        rank = jnp.int32(0)
        for i in range(j):
            rank = rank + (shifts[i] == shifts[j]).astype(jnp.int32)
        ranks.append(rank)
    for s in range(NZ):
        for r in range(CAP):
            pick = jnp.int32(0)
            for j in range(TPD):
                pick = jnp.where((shifts[j] == s) & (ranks[j] == r), j, pick)
            sends[s][r] = q[pl.ds(pl.multiple_of(pick * TILE, TILE), TILE), :]
    for s in range(NZ):
        base = (leaf * NZ + ((ctx - s) & (NZ - 1))) * TPD
        table[s * CAP] = jnp.int32(-1)
        table[s * CAP + 1] = jnp.int32(-1)

        def one(j, rank, s=s, base=base):
            to = dest[base + j]
            mine = (to >> 3) == device

            @pl.when(mine)
            def _():
                table[s * CAP + rank] = to & (TPD - 1)
                info[to & (TPD - 1)] = base + j

            return rank + mine.astype(jnp.int32)

        lax.fori_loop(0, TPD, one, jnp.int32(0))


def pack(where, dest, q):
    width = q.shape[1]
    outs = pl.pallas_call(
        pack_kernel,
        in_specs=[smem(), smem(), vmem()],
        out_specs=[vmem()] * NZ + [smem(), smem()],
        out_shape=[jax.ShapeDtypeStruct((CAP, TILE, width), q.dtype)] * NZ
        + [jax.ShapeDtypeStruct((NZ * CAP,), jnp.int32), jax.ShapeDtypeStruct((TPD,), jnp.int32)],
        compiler_params=pltpu.CompilerParams(vmem_limit_bytes=32 * MIB),
        cost_estimate=pl.CostEstimate(flops=0, bytes_accessed=3 * MIB, transcendentals=0),
        name="pack",
    )(where, dest, q)
    return outs[:NZ], outs[NZ], outs[NZ + 1]


def walk_kernel(parents, info, which, place, lists, tiles, counts):
    for p in range(PASSES):
        counts[p] = jnp.int32(0)

    def tile(d, carry):
        seg = info[d] >> 2

        def body(at):
            p = which[at]
            used = counts[p]

            @pl.when((used & (UNIT - 1)) == 0)
            def _():
                tiles[p * ITEMS + used // UNIT] = d + jnp.where(at == seg, TPD, 0)

            lists[p * ITEMS * UNIT + used] = place[at]
            counts[p] = used + 1
            return parents[at]

        lax.while_loop(lambda at: at >= 0, body, seg)
        for p in range(PASSES):
            used = counts[p]
            for n in range(UNIT):
                lists[p * ITEMS * UNIT + used + n] = jnp.int32(-1)
            counts[p] = ((used + UNIT - 1) // UNIT) * UNIT
        return carry

    lax.fori_loop(0, TPD, tile, 0)
    for p in range(PASSES):
        used = counts[p]
        tiles[p * ITEMS + used // UNIT] = jnp.int32(0)
        for n in range(UNIT):
            lists[p * ITEMS * UNIT + used + n] = jnp.int32(-1)


def walk(parents, info, which, place):
    return pl.pallas_call(
        walk_kernel,
        in_specs=[smem()] * 4,
        out_specs=[smem()] * 3,
        out_shape=[
            jax.ShapeDtypeStruct((PASSES * ITEMS * UNIT,), jnp.int32),
            jax.ShapeDtypeStruct((PASSES * ITEMS,), jnp.int32),
            jax.ShapeDtypeStruct((PASSES,), jnp.int32),
        ],
        cost_estimate=pl.CostEstimate(flops=0, bytes_accessed=16 * MIB, transcendentals=0),
        name="walk",
    )(parents, info, which, place)


def unpack_kernel(table, *refs):
    came, out = refs[:NZ], refs[NZ]
    for s in range(NZ):

        def one(r, carry, s=s):
            d = table[s * CAP + r]

            @pl.when(d >= 0)
            def _():
                for g in range(2):
                    heads = [
                        came[s][r, :, pl.ds((g * GROUP + h) * HEAD, HEAD)] for h in range(GROUP)
                    ]
                    out[d, g] = jnp.concatenate(heads, axis=0).T

            return carry

        lax.fori_loop(0, CAP, one, 0)


def unpack(table, came):
    return pl.pallas_call(
        unpack_kernel,
        in_specs=[smem()] + [vmem()] * NZ,
        out_specs=vmem(),
        out_shape=jax.ShapeDtypeStruct((TPD, 2, HEAD, ROWS), jnp.bfloat16),
        compiler_params=pltpu.CompilerParams(vmem_limit_bytes=32 * MIB),
        cost_estimate=pl.CostEstimate(flops=0, bytes_accessed=6 * MIB, transcendentals=0),
        name="unpack",
    )(table, *came)


def project_kernel(where, own, before, after, far0, far1, wk, wv, out):
    y = where[2]
    depth = own.shape[1]
    half = far0.shape[0]

    def rows(by):
        at = (y + by) & (NY - 1)
        return pl.ds(pl.multiple_of(at * depth, depth), depth)

    def times(w):
        total = jnp.dot(own[...], w[rows(0), :], preferred_element_type=jnp.float32)
        total += jnp.dot(before[...], w[rows(NY - 1), :], preferred_element_type=jnp.float32)
        total += jnp.dot(after[...], w[rows(1), :], preferred_element_type=jnp.float32)
        far = jnp.concatenate([far0[...], far1[...]], axis=0)
        return total + jnp.dot(far, w[rows(2), :], preferred_element_type=jnp.float32)

    k = times(wk)
    v = times(wv)
    for n in range(2):
        at = n * 2 * SEG
        out[at : at + SEG, :] = k[n * SEG : (n + 1) * SEG].astype(out.dtype)
        for g in range(2):
            part = v[n * SEG : (n + 1) * SEG, g * HEAD : (g + 1) * HEAD]
            out[at + SEG : at + 2 * SEG, g * HEAD : (g + 1) * HEAD] = part.T.astype(out.dtype)


def project(where, own, before, after, far0, far1, wk, wv):
    return pl.pallas_call(
        project_kernel,
        in_specs=[smem()] + [vmem()] * 7,
        out_specs=vmem(),
        out_shape=jax.ShapeDtypeStruct((4 * SEG, 2 * HEAD), jnp.bfloat16),
        compiler_params=pltpu.CompilerParams(vmem_limit_bytes=40 * MIB),
        cost_estimate=pl.CostEstimate(flops=2 * 256 * 5120 * 512, bytes_accessed=8 * MIB, transcendentals=0),
        name="project",
    )(where, own, before, after, far0, far1, wk, wv)


def attend_kernel(which, n_pieces, lists, tiles, counts, info, qt, *refs):
    pieces, refs = refs[:n_pieces], refs[n_pieces:]
    first, finish = which == 0, which == PASSES - 1
    if not first:
        refs = refs[3:]
    top, total, acc = refs[:3]
    if finish:
        out, kv, score, peak, weight, sems = refs[3:]
    else:
        kv, score, peak, weight, sems = refs[3:]
    copies, at = [], 0
    for n, piece in enumerate(pieces):
        size = piece.shape[0]
        copies.append(pltpu.make_async_copy(piece, kv.at[pl.ds(at, size)], sems.at[n]))
        at += size
    for copy in copies:
        copy.start()
    if first:
        top[...] = jnp.full(top.shape, FILL, jnp.float32)
        total[...] = jnp.zeros(total.shape, jnp.float32)
        acc[...] = jnp.zeros(acc.shape, jnp.float32)
    weight[...] = jnp.zeros(weight.shape, weight.dtype)
    for copy in copies:
        copy.wait()

    def entries(j):
        return [lists[(which * ITEMS + j) * UNIT + u] for u in range(UNIT)]

    def places(j):
        return [jnp.maximum(e, 0) for e in entries(j)]

    def tile_of(j):
        return tiles[which * ITEMS + j] & (TPD - 1)

    def scores(j):
        d, spots = tile_of(j), places(j)
        for g in range(2):
            k = jnp.concatenate([kv[w, 0:SEG, g * HEAD : (g + 1) * HEAD] for w in spots], axis=0)
            s = jnp.dot(k, qt[d, g], preferred_element_type=jnp.float32)
            score[g] = s
            for u in range(UNIT):
                part = s[u * SEG : (u + 1) * SEG].reshape(SEG // 8, 8, ROWS)
                peak[g, u] = jnp.max(part, axis=0)

        @pl.when(tiles[which * ITEMS + j] >= TPD)
        def _():
            key = lax.broadcasted_iota(jnp.int32, (SEG, ROWS), 0)
            token = lax.broadcasted_iota(jnp.int32, (SEG, ROWS), 1) & (TILE - 1)
            ok = key <= token + (info[d] & 3) * TILE
            for g in range(2):
                s = jnp.where(ok, score[g, 0:SEG], FILL)
                score[g, 0:SEG] = s
                peak[g, 0] = jnp.max(s.reshape(SEG // 8, 8, ROWS), axis=0)

    def add(j, drops):
        d, spots = tile_of(j), places(j)
        for g in range(2):
            v = jnp.concatenate(
                [kv[w, SEG : 2 * SEG, g * HEAD : (g + 1) * HEAD] for w in spots], axis=1
            )
            acc[d * 2 + g] = acc[d * 2 + g] * drops[g] + jnp.dot(
                v, weight[g], preferred_element_type=jnp.float32
            )

    def body(j, drops):
        add(jnp.maximum(j - 1, 0), drops)
        d = tile_of(j)
        pens = [jnp.where(e < 0, 3e31, 0.0) for e in entries(j)]
        result = []
        for g in range(2):
            i = d * 2 + g
            old = top[i]
            peaks = functools.reduce(jnp.maximum, [peak[g, u] - pens[u] for u in range(UNIT)])
            new = jnp.maximum(old, jnp.max(peaks, axis=0, keepdims=True))
            drop = jnp.exp2((old - new) * SCALE)
            part = jnp.zeros((8, ROWS), jnp.float32)
            for u in range(UNIT):
                e = jnp.exp2((score[g, u * SEG : (u + 1) * SEG] - (new + pens[u])) * SCALE)
                part += jnp.sum(e.reshape(SEG // 8, 8, ROWS), axis=0)
                weight[g, u * SEG : (u + 1) * SEG] = e.astype(jnp.bfloat16)
            total[i] = total[i] * drop + jnp.sum(part, axis=0, keepdims=True)
            top[i] = new
            result.append(drop)
        scores(j + 1)
        return tuple(result)

    rounds = counts[which] // UNIT
    ones = jnp.ones((1, ROWS), jnp.float32)
    scores(0)
    drops = lax.fori_loop(0, rounds, body, (ones, ones))
    add(jnp.maximum(rounds - 1, 0), drops)

    if finish:

        def write(d, carry):
            for g in range(2):
                i = d * 2 + g
                o = (acc[i] / total[i]).T.astype(out.dtype)
                for h in range(GROUP):
                    out[
                        pl.ds(pl.multiple_of(d * TILE, TILE), TILE),
                        (g * GROUP + h) * HEAD : (g * GROUP + h + 1) * HEAD,
                    ] = o[h * TILE : (h + 1) * TILE]
            return carry

        lax.fori_loop(0, TPD, write, 0)


def attend(which, work, qt, pieces, state):
    first, finish = which == 0, which == PASSES - 1
    shapes = [
        jax.ShapeDtypeStruct((2 * TPD, 1, ROWS), jnp.float32),
        jax.ShapeDtypeStruct((2 * TPD, 1, ROWS), jnp.float32),
        jax.ShapeDtypeStruct((2 * TPD, HEAD, ROWS), jnp.float32),
    ]
    if finish:
        shapes.append(jax.ShapeDtypeStruct((TPD * TILE, 2 * GROUP * HEAD), jnp.bfloat16))
    blocks = sum(piece.shape[0] for piece in pieces)
    begin = len(work) + 1 + len(pieces)
    return pl.pallas_call(
        functools.partial(attend_kernel, which, len(pieces)),
        in_specs=[smem()] * len(work)
        + [vmem()]
        + [pl.BlockSpec(memory_space=pl.ANY)] * len(pieces)
        + [vmem()] * (0 if first else 3),
        out_specs=[vmem()] * len(shapes),
        out_shape=shapes,
        input_output_aliases={} if first else {begin + n: n for n in range(3)},
        scratch_shapes=[
            pltpu.VMEM((blocks, 2 * SEG, 2 * HEAD), jnp.bfloat16),
            pltpu.VMEM((2, UNIT * SEG, ROWS), jnp.float32),
            pltpu.VMEM((2, UNIT, 8, ROWS), jnp.float32),
            pltpu.VMEM((2, UNIT * SEG, ROWS), jnp.bfloat16),
            pltpu.SemaphoreType.DMA((len(pieces),)),
        ],
        compiler_params=pltpu.CompilerParams(vmem_limit_bytes=28 * MIB),
        cost_estimate=pl.CostEstimate(
            flops=256 * 16 * 128 * 128 * 32, bytes_accessed=6 * MIB, transcendentals=0
        ),
        name="attend",
    )(*work, qt, *pieces, *(() if first else state))


def cat(*parts):
    return jnp.concatenate(parts, axis=0)


def ring_four(block, axis, up, down, also=()):
    half = block.shape[0] // 2
    low = lax.ppermute(block, axis, up)
    high = lax.ppermute(block, axis, down)
    low, high, also = lax.optimization_barrier((low, high, also))
    far0 = lax.ppermute(low[:half], axis, up)
    far1 = lax.ppermute(high[half:], axis, down)
    return [block, low, high, far0, far1], also


def along_z(a, b):
    return lax.ppermute(a, "ctx", ZP), lax.ppermute(b, "ctx", ZM)


def swap(a):
    return lax.ppermute(a, "leaf", CS)


def swapped(*pieces):
    return in_blocks(list(pieces) + [swap(a) for a in pieces])


def in_blocks(pieces):
    return [a.reshape(-1, 2 * SEG, 2 * HEAD) for a in pieces]


def on_device(queries, inputs, key_weight, value_weight, parents, tile_dest):
    leaf, ctx, y = lax.axis_index("leaf"), lax.axis_index("ctx"), lax.axis_index("head")
    where = jnp.stack([leaf, ctx, y]).astype(jnp.int32)
    sends, table, info = pack(where, tile_dest, queries)
    came = {0: sends[0]}
    for s in (1, 7, 4, 3, 5, 6, 2):
        came[s] = lax.ppermute(sends[s], "ctx", turn(NZ, s))
    rows, (came[1], came[7]) = ring_four(inputs, "head", YP, YM, (came[1], came[7]))

    seg = jnp.arange(parents.shape[0], dtype=jnp.int32)
    block = seg >> 1
    from_leaf, from_z = block >> 3, block & (NZ - 1)
    z = (from_z - ctx) & (NZ - 1)
    x = ((from_leaf >> 1) - (leaf >> 1)) & (NX - 1)
    at_x = jnp.where(x == 0, 0, jnp.where(x == 1, 2, jnp.where(x == 2, 3, 1)))
    which = jnp.where(z <= 4, z, NZ - z)
    ahead = jnp.where((z > 0) & (z < 4), 8, 0)
    span = jnp.where((which == 0) | (which == 4), 8, 16)
    place = at_x * 2 + (seg & 1) + ahead + span * ((from_leaf ^ leaf) & 1)
    work = list(walk(parents, info, which, place))
    rows, work, came[4], came[3] = lax.optimization_barrier((rows, work, came[4], came[3]))
    work.append(info)

    kv = project(where, *rows, key_weight, value_weight)
    plane = cat(*ring_four(kv, "leaf", XP, XM)[0])
    plane, came[2], came[5], came[6] = lax.optimization_barrier(
        (plane, came[2], came[5], came[6])
    )
    qt = unpack(table, [came[s] for s in range(NZ)])

    low, high = along_z(plane, plane)
    state = attend(0, work, qt, swapped(plane), None)
    for p in range(1, PASSES - 1):
        low, high, state = lax.optimization_barrier((low, high, state))
        pieces = swapped(low, high)
        if p == PASSES - 2:
            half = plane.shape[0] // 2
            low, high = low[:half], high[half:]
        low, high = along_z(low, high)
        state = attend(p, work, qt, pieces, state)
    low, high, state = lax.optimization_barrier((low, high, state))
    return attend(PASSES - 1, work, qt, swapped(low, high), state)[3]


def solution(mesh):
    in_specs = (
        P(("leaf", "ctx"), "head"),
        P(("leaf", "ctx"), "head"),
        P(None, "head"),
        P(None, "head"),
        P(),
        P(),
    )
    out_specs = P(("leaf", "ctx"), "head")
    return jax.shard_map(
        on_device, mesh=mesh, in_specs=in_specs, out_specs=out_specs, check_vma=False
    )
```

```python
import functools
import math

import jax
import jax.numpy as jnp
from jax import lax
from jax.experimental import pallas as pl
from jax.experimental.pallas import tpu as pltpu
from jax.sharding import PartitionSpec as P

HEAD = 128
GROUP = 8
SEG = 128
TILE = 32
TPD = 8
CAP = 2
NX, NZ, NY = 4, 8, 4
ROWS = TILE * GROUP
SCALE = math.log2(math.e) / math.sqrt(HEAD)
FILL = -1.2e31
MIB = 1 << 20
UNIT = 4
PASSES = 5
ITEMS = 8 * 32 // UNIT + 4

XP = [(2 * x + c, 2 * ((x + 1) % NX) + c) for x in range(NX) for c in range(2)]
XM = [(2 * x + c, 2 * ((x - 1) % NX) + c) for x in range(NX) for c in range(2)]
CS = [(i, i ^ 1) for i in range(2 * NX)]


def turn(n, by):
    return [(i, (i + by) % n) for i in range(n)]


ZP, ZM = turn(NZ, 1), turn(NZ, -1)
YP, YM = turn(NY, 1), turn(NY, -1)

smem = functools.partial(pl.BlockSpec, memory_space=pltpu.SMEM)
vmem = functools.partial(pl.BlockSpec, memory_space=pltpu.VMEM)


def pack_kernel(where, dest, q, *outs):
    sends, table, info = outs[:NZ], outs[NZ], outs[NZ + 1]
    leaf, ctx = where[0], where[1]
    device = leaf * NZ + ctx
    shifts = [((dest[device * TPD + j] >> 3) - ctx) & (NZ - 1) for j in range(TPD)]
    ranks = []
    for j in range(TPD):
        rank = jnp.int32(0)
        for i in range(j):
            rank = rank + (shifts[i] == shifts[j]).astype(jnp.int32)
        ranks.append(rank)
    for s in range(NZ):
        for r in range(CAP):
            pick = jnp.int32(0)
            for j in range(TPD):
                pick = jnp.where((shifts[j] == s) & (ranks[j] == r), j, pick)
            sends[s][r] = q[pl.ds(pl.multiple_of(pick * TILE, TILE), TILE), :]
    for s in range(NZ):
        base = (leaf * NZ + ((ctx - s) & (NZ - 1))) * TPD
        table[s * CAP] = jnp.int32(-1)
        table[s * CAP + 1] = jnp.int32(-1)

        def one(j, rank, s=s, base=base):
            to = dest[base + j]
            mine = (to >> 3) == device

            @pl.when(mine)
            def _():
                table[s * CAP + rank] = to & (TPD - 1)
                info[to & (TPD - 1)] = base + j

            return rank + mine.astype(jnp.int32)

        lax.fori_loop(0, TPD, one, jnp.int32(0))


def pack(where, dest, q):
    width = q.shape[1]
    outs = pl.pallas_call(
        pack_kernel,
        in_specs=[smem(), smem(), vmem()],
        out_specs=[vmem()] * NZ + [smem(), smem()],
        out_shape=[jax.ShapeDtypeStruct((CAP, TILE, width), q.dtype)] * NZ
        + [jax.ShapeDtypeStruct((NZ * CAP,), jnp.int32), jax.ShapeDtypeStruct((TPD,), jnp.int32)],
        compiler_params=pltpu.CompilerParams(vmem_limit_bytes=32 * MIB),
        cost_estimate=pl.CostEstimate(flops=0, bytes_accessed=3 * MIB, transcendentals=0),
        name="pack",
    )(where, dest, q)
    return outs[:NZ], outs[NZ], outs[NZ + 1]


def walk_kernel(parents, info, which, place, lists, tiles, counts):
    for p in range(PASSES):
        counts[p] = jnp.int32(0)

    def tile(d, carry):
        seg = info[d] >> 2

        def body(at):
            p = which[at]
            used = counts[p]

            @pl.when((used & (UNIT - 1)) == 0)
            def _():
                tiles[p * ITEMS + used // UNIT] = d + jnp.where(at == seg, TPD, 0)

            lists[p * ITEMS * UNIT + used] = place[at]
            counts[p] = used + 1
            return parents[at]

        lax.while_loop(lambda at: at >= 0, body, seg)
        for p in range(PASSES):
            used = counts[p]
            for n in range(UNIT):
                lists[p * ITEMS * UNIT + used + n] = jnp.int32(-1)
            counts[p] = ((used + UNIT - 1) // UNIT) * UNIT
        return carry

    lax.fori_loop(0, TPD, tile, 0)
    for p in range(PASSES):
        used = counts[p]
        tiles[p * ITEMS + used // UNIT] = jnp.int32(0)
        for n in range(UNIT):
            lists[p * ITEMS * UNIT + used + n] = jnp.int32(-1)


def walk(parents, info, which, place):
    return pl.pallas_call(
        walk_kernel,
        in_specs=[smem()] * 4,
        out_specs=[smem()] * 3,
        out_shape=[
            jax.ShapeDtypeStruct((PASSES * ITEMS * UNIT,), jnp.int32),
            jax.ShapeDtypeStruct((PASSES * ITEMS,), jnp.int32),
            jax.ShapeDtypeStruct((PASSES,), jnp.int32),
        ],
        cost_estimate=pl.CostEstimate(flops=0, bytes_accessed=16 * MIB, transcendentals=0),
        name="walk",
    )(parents, info, which, place)


def unpack_kernel(table, *refs):
    came, out = refs[:NZ], refs[NZ]
    for s in range(NZ):

        def one(r, carry, s=s):
            d = table[s * CAP + r]

            @pl.when(d >= 0)
            def _():
                for g in range(2):
                    heads = [
                        came[s][r, :, pl.ds((g * GROUP + h) * HEAD, HEAD)] for h in range(GROUP)
                    ]
                    out[d, g] = jnp.concatenate(heads, axis=0).T

            return carry

        lax.fori_loop(0, CAP, one, 0)


def unpack(table, came):
    return pl.pallas_call(
        unpack_kernel,
        in_specs=[smem()] + [vmem()] * NZ,
        out_specs=vmem(),
        out_shape=jax.ShapeDtypeStruct((TPD, 2, HEAD, ROWS), jnp.bfloat16),
        compiler_params=pltpu.CompilerParams(vmem_limit_bytes=32 * MIB),
        cost_estimate=pl.CostEstimate(flops=0, bytes_accessed=6 * MIB, transcendentals=0),
        name="unpack",
    )(table, *came)


def project_kernel(where, own, before, after, far0, far1, wk, wv, out):
    y = where[2]
    depth = own.shape[1]
    half = far0.shape[0]

    def rows(by):
        at = (y + by) & (NY - 1)
        return pl.ds(pl.multiple_of(at * depth, depth), depth)

    def times(w):
        total = jnp.dot(own[...], w[rows(0), :], preferred_element_type=jnp.float32)
        total += jnp.dot(before[...], w[rows(NY - 1), :], preferred_element_type=jnp.float32)
        total += jnp.dot(after[...], w[rows(1), :], preferred_element_type=jnp.float32)
        far = jnp.concatenate([far0[...], far1[...]], axis=0)
        return total + jnp.dot(far, w[rows(2), :], preferred_element_type=jnp.float32)

    k = times(wk)
    v = times(wv)
    for n in range(2):
        at = n * 2 * SEG
        out[at : at + SEG, :] = k[n * SEG : (n + 1) * SEG].astype(out.dtype)
        for g in range(2):
            part = v[n * SEG : (n + 1) * SEG, g * HEAD : (g + 1) * HEAD]
            out[at + SEG : at + 2 * SEG, g * HEAD : (g + 1) * HEAD] = part.T.astype(out.dtype)


def project(where, own, before, after, far0, far1, wk, wv):
    return pl.pallas_call(
        project_kernel,
        in_specs=[smem()] + [vmem()] * 7,
        out_specs=vmem(),
        out_shape=jax.ShapeDtypeStruct((4 * SEG, 2 * HEAD), jnp.bfloat16),
        compiler_params=pltpu.CompilerParams(vmem_limit_bytes=40 * MIB),
        cost_estimate=pl.CostEstimate(flops=2 * 256 * 5120 * 512, bytes_accessed=8 * MIB, transcendentals=0),
        name="project",
    )(where, own, before, after, far0, far1, wk, wv)


def attend_kernel(which, n_pieces, lists, tiles, counts, info, qt, *refs):
    pieces, refs = refs[:n_pieces], refs[n_pieces:]
    first, finish = which == 0, which == PASSES - 1
    if not first:
        refs = refs[3:]
    top, total, acc = refs[:3]
    if finish:
        out, kv, score, peak, weight, sems = refs[3:]
    else:
        kv, score, peak, weight, sems = refs[3:]
    copies, at = [], 0
    for n, piece in enumerate(pieces):
        size = piece.shape[0]
        copies.append(pltpu.make_async_copy(piece, kv.at[pl.ds(at, size)], sems.at[n]))
        at += size
    for copy in copies:
        copy.start()
    if first:
        top[...] = jnp.full(top.shape, FILL, jnp.float32)
        total[...] = jnp.zeros(total.shape, jnp.float32)
        acc[...] = jnp.zeros(acc.shape, jnp.float32)
    weight[...] = jnp.zeros(weight.shape, weight.dtype)
    for copy in copies:
        copy.wait()

    def entries(j):
        return [lists[(which * ITEMS + j) * UNIT + u] for u in range(UNIT)]

    def places(j):
        return [jnp.maximum(e, 0) for e in entries(j)]

    def tile_of(j):
        return tiles[which * ITEMS + j] & (TPD - 1)

    def scores(j):
        d, spots = tile_of(j), places(j)
        for g in range(2):
            k = jnp.concatenate([kv[w, 0:SEG, g * HEAD : (g + 1) * HEAD] for w in spots], axis=0)
            s = jnp.dot(k, qt[d, g], preferred_element_type=jnp.float32)
            score[g] = s
            for u in range(UNIT):
                part = s[u * SEG : (u + 1) * SEG].reshape(SEG // 8, 8, ROWS)
                peak[g, u] = jnp.max(part, axis=0)

        @pl.when(tiles[which * ITEMS + j] >= TPD)
        def _():
            key = lax.broadcasted_iota(jnp.int32, (SEG, ROWS), 0)
            token = lax.broadcasted_iota(jnp.int32, (SEG, ROWS), 1) & (TILE - 1)
            ok = key <= token + (info[d] & 3) * TILE
            for g in range(2):
                s = jnp.where(ok, score[g, 0:SEG], FILL)
                score[g, 0:SEG] = s
                peak[g, 0] = jnp.max(s.reshape(SEG // 8, 8, ROWS), axis=0)

    def add(j, drops):
        d, spots = tile_of(j), places(j)
        for g in range(2):
            v = jnp.concatenate(
                [kv[w, SEG : 2 * SEG, g * HEAD : (g + 1) * HEAD] for w in spots], axis=1
            )
            acc[d * 2 + g] = acc[d * 2 + g] * drops[g] + jnp.dot(
                v, weight[g], preferred_element_type=jnp.float32
            )

    def body(j, drops):
        add(jnp.maximum(j - 1, 0), drops)
        d = tile_of(j)
        pens = [jnp.where(e < 0, 3e31, 0.0) for e in entries(j)]
        result = []
        for g in range(2):
            i = d * 2 + g
            old = top[i]
            peaks = functools.reduce(jnp.maximum, [peak[g, u] - pens[u] for u in range(UNIT)])
            new = jnp.maximum(old, jnp.max(peaks, axis=0, keepdims=True))
            drop = jnp.exp2((old - new) * SCALE)
            part = jnp.zeros((8, ROWS), jnp.float32)
            for u in range(UNIT):
                e = jnp.exp2((score[g, u * SEG : (u + 1) * SEG] - (new + pens[u])) * SCALE)
                part += jnp.sum(e.reshape(SEG // 8, 8, ROWS), axis=0)
                weight[g, u * SEG : (u + 1) * SEG] = e.astype(jnp.bfloat16)
            total[i] = total[i] * drop + jnp.sum(part, axis=0, keepdims=True)
            top[i] = new
            result.append(drop)
        scores(j + 1)
        return tuple(result)

    rounds = counts[which] // UNIT
    ones = jnp.ones((1, ROWS), jnp.float32)
    scores(0)
    drops = lax.fori_loop(0, rounds, body, (ones, ones))
    add(jnp.maximum(rounds - 1, 0), drops)

    if finish:

        def write(d, carry):
            for g in range(2):
                i = d * 2 + g
                o = (acc[i] / total[i]).T.astype(out.dtype)
                for h in range(GROUP):
                    out[
                        pl.ds(pl.multiple_of(d * TILE, TILE), TILE),
                        (g * GROUP + h) * HEAD : (g * GROUP + h + 1) * HEAD,
                    ] = o[h * TILE : (h + 1) * TILE]
            return carry

        lax.fori_loop(0, TPD, write, 0)


def attend(which, work, qt, pieces, state):
    first, finish = which == 0, which == PASSES - 1
    shapes = [
        jax.ShapeDtypeStruct((2 * TPD, 1, ROWS), jnp.float32),
        jax.ShapeDtypeStruct((2 * TPD, 1, ROWS), jnp.float32),
        jax.ShapeDtypeStruct((2 * TPD, HEAD, ROWS), jnp.float32),
    ]
    if finish:
        shapes.append(jax.ShapeDtypeStruct((TPD * TILE, 2 * GROUP * HEAD), jnp.bfloat16))
    blocks = sum(piece.shape[0] for piece in pieces)
    begin = len(work) + 1 + len(pieces)
    return pl.pallas_call(
        functools.partial(attend_kernel, which, len(pieces)),
        in_specs=[smem()] * len(work)
        + [vmem()]
        + [pl.BlockSpec(memory_space=pl.ANY)] * len(pieces)
        + [vmem()] * (0 if first else 3),
        out_specs=[vmem()] * len(shapes),
        out_shape=shapes,
        input_output_aliases={} if first else {begin + n: n for n in range(3)},
        scratch_shapes=[
            pltpu.VMEM((blocks, 2 * SEG, 2 * HEAD), jnp.bfloat16),
            pltpu.VMEM((2, UNIT * SEG, ROWS), jnp.float32),
            pltpu.VMEM((2, UNIT, 8, ROWS), jnp.float32),
            pltpu.VMEM((2, UNIT * SEG, ROWS), jnp.bfloat16),
            pltpu.SemaphoreType.DMA((len(pieces),)),
        ],
        compiler_params=pltpu.CompilerParams(vmem_limit_bytes=28 * MIB),
        cost_estimate=pl.CostEstimate(
            flops=256 * 16 * 128 * 128 * 32, bytes_accessed=6 * MIB, transcendentals=0
        ),
        name="attend",
    )(*work, qt, *pieces, *(() if first else state))


def cat(*parts):
    return jnp.concatenate(parts, axis=0)


def ring_four(block, axis, up, down, also=()):
    half = block.shape[0] // 2
    low = lax.ppermute(block, axis, up)
    high = lax.ppermute(block, axis, down)
    low, high, also = lax.optimization_barrier((low, high, also))
    far0 = lax.ppermute(low[:half], axis, up)
    far1 = lax.ppermute(high[half:], axis, down)
    return [block, low, high, far0, far1], also


def along_z(a, b):
    return lax.ppermute(a, "ctx", ZP), lax.ppermute(b, "ctx", ZM)


def swap(a):
    return lax.ppermute(a, "leaf", CS)


def swapped(*pieces):
    return in_blocks(list(pieces) + [swap(a) for a in pieces])


def in_blocks(pieces):
    return [a.reshape(-1, 2 * SEG, 2 * HEAD) for a in pieces]


def on_device(queries, inputs, key_weight, value_weight, parents, tile_dest):
    leaf, ctx, y = lax.axis_index("leaf"), lax.axis_index("ctx"), lax.axis_index("head")
    where = jnp.stack([leaf, ctx, y]).astype(jnp.int32)
    sends, table, info = pack(where, tile_dest, queries)
    came = {0: sends[0]}
    for s in range(1, NZ):
        came[s] = lax.ppermute(sends[s], "ctx", turn(NZ, s))
    rows, _ = ring_four(inputs, "head", YP, YM, sends)

    seg = jnp.arange(parents.shape[0], dtype=jnp.int32)
    block = seg >> 1
    from_leaf, from_z = block >> 3, block & (NZ - 1)
    z = (from_z - ctx) & (NZ - 1)
    x = ((from_leaf >> 1) - (leaf >> 1)) & (NX - 1)
    at_x = jnp.where(x == 0, 0, jnp.where(x == 1, 2, jnp.where(x == 2, 3, 1)))
    which = jnp.where(z <= 4, z, NZ - z)
    ahead = jnp.where((z > 0) & (z < 4), 8, 0)
    span = jnp.where((which == 0) | (which == 4), 8, 16)
    place = at_x * 2 + (seg & 1) + ahead + span * ((from_leaf ^ leaf) & 1)
    work = list(walk(parents, info, which, place))
    rows, work = lax.optimization_barrier((rows, work))
    work.append(info)

    kv = project(where, *rows, key_weight, value_weight)
    plane = cat(*ring_four(kv, "leaf", XP, XM)[0])
    qt = unpack(table, [came[s] for s in range(NZ)])
    plane, qt = lax.optimization_barrier((plane, qt))

    low, high = along_z(plane, plane)
    state = attend(0, work, qt, swapped(plane), None)
    for p in range(1, PASSES - 1):
        low, high, state = lax.optimization_barrier((low, high, state))
        pieces = swapped(low, high)
        if p == PASSES - 2:
            half = plane.shape[0] // 2
            low, high = low[:half], high[half:]
        low, high = along_z(low, high)
        state = attend(p, work, qt, pieces, state)
    low, high, state = lax.optimization_barrier((low, high, state))
    return attend(PASSES - 1, work, qt, swapped(low, high), state)[3]


def solution(mesh):
    in_specs = (
        P(("leaf", "ctx"), "head"),
        P(("leaf", "ctx"), "head"),
        P(None, "head"),
        P(None, "head"),
        P(),
        P(),
    )
    out_specs = P(("leaf", "ctx"), "head")
    return jax.shard_map(
        on_device, mesh=mesh, in_specs=in_specs, out_specs=out_specs, check_vma=False
    )
```
